32 devices in a mesh: dev: 4 (over y, x), gx: 4 (over z), gy: 2 (over core).
Axes of the slice: x: 2, y: 2, z: 4, core: 2. Of those that a mesh axis runs over, the one named last changes fastest.
Arguments:
- tokens: bfloat16 [4096, 1024], P(('dev', 'gy'), 'gx'), may hold values from -6 to 6
- norm_gain: bfloat16 [1024], P('gx'), may hold values from 0.099609375 to 1.8984375
- w_query: bfloat16 [1024, 2048], P('gy', 'gx'), may hold values from -0.1875 to 0.1875
- key_projection: bfloat16 [1024, 1024], P('gy', 'gx'), may hold values from -0.1875 to 0.1875
- value_projection: bfloat16 [1024, 1024], P('gy', 'gx'), may hold values from -0.1875 to 0.1875
- query_gain: bfloat16 [128], replicated, may hold values from 0.099609375 to 1.8984375
- key_gain: bfloat16 [128], replicated, may hold values from 0.099609375 to 1.8984375
- w_out: bfloat16 [2048, 1024], P('gx', 'gy'), may hold values from -0.5 to 0.5
- ffn_gain: bfloat16 [1024], P('gx'), may hold values from 0.099609375 to 1.8984375
- w_gate: bfloat16 [1024, 3072], P('gy', 'gx'), may hold values from -0.1875 to 0.1875
- w_up: bfloat16 [1024, 3072], P('gy', 'gx'), may hold values from -0.1875 to 0.1875
- w_down: bfloat16 [3072, 1024], P('gx', 'gy'), may hold values from -0.109375 to 0.109375
- cotangent: bfloat16 [4096, 1024], P(('dev', 'gy'), 'gx'), may hold values from -6 to 6
- sequence: int32 [4096], P('dev'), may hold values from 0 to 1, as said below
- position: int32 [4096], P('dev'), may hold values from 0 to 959, as said below
Outputs:
- output: bfloat16 [4096, 1024], P(('dev', 'gy'), 'gx')
- grad_tokens: float32 [4096, 1024], P(('dev', 'gy'), 'gx')
- grad_norm_gain: float32 [1024], P('gx')
- grad_query: float32 [1024, 2048], P('gy', 'gx')
- grad_key: float32 [1024, 1024], P('gy', 'gx')
- grad_value: float32 [1024, 1024], P('gy', 'gx')
- grad_query_gain: float32 [128], replicated
- grad_key_gain: float32 [128], replicated
- grad_out: float32 [2048, 1024], P('gx', 'gy')
- grad_ffn_gain: float32 [1024], P('gx')
- grad_gate: float32 [1024, 3072], P('gy', 'gx')
- grad_up: float32 [1024, 3072], P('gy', 'gx')
- grad_down: float32 [3072, 1024], P('gx', 'gy')
The draws below stay inside these ranges and needn't reach their ends.
Inputs may be any that keep to these rules, and one draw needn't show every extreme that they name: Each index of dev holds a block of 1024 tokens read as a stream: token t of the stream lies in row (t mod g) * 512 + floor(t / g) of the block, g = 2. Along the stream the numbers start at 0 and rise by one at each new sequence. One sequence of each block has 960 tokens; every other one has 64 tokens. `position`: the place of each token in its sequence along the stream, 0 at its first token.
All inputs are finite; a program needn't handle non-finite values.
Results may differ from the reference program's by a relative error of at most 0.024.
Values may be sent and summed in bfloat16 or wider, within the bound.
No kernel may reach another device: no remote copies, remote signals or barrier semaphores. Data moves between devices by JAX's collectives and lax.ppermute only.
A program may use at most 256 MiB of HBM per device.

```python
import jax
import jax.numpy as jnp
from jax import lax

MODEL_WIDTH = 1024
QUERY_HEADS = 16
KEY_VALUE_HEADS = 8
HEAD_SIZE = 128
FF = 3072
ROWS = 512
SHORT = 64
GROUP = 1024
LEN = 960
TOKENS = 4096


def stream_layout(key):
    blocks = TOKENS // GROUP
    grain = SHORT
    start_key = jax.random.fold_in(key, 11)
    starts = jax.random.randint(start_key, (blocks, 1), 0, (GROUP - LEN) // grain + 1) * grain
    stream = jnp.arange(GROUP, dtype=jnp.int32)[None, :]
    inside = (stream > starts) & (stream < starts + LEN)
    cuts = (stream % grain == 0) & ~inside & (stream > 0)
    number = jnp.cumsum(cuts.astype(jnp.int32), axis=1)
    first = lax.cummax(jnp.where(cuts, stream, 0), axis=1)
    offset = stream - first
    row_index = jnp.arange(GROUP, dtype=jnp.int32)
    order = row_index % ROWS * (GROUP // ROWS) + row_index // ROWS
    return (number[:, order].reshape(-1), offset[:, order].reshape(-1))


def draw_sequence(key, part):
    shared = stream_layout(key)
    return shared[0]


def draw_position(key, part):
    shared = stream_layout(key)
    return shared[1]


def block_scale(key, dims, cuts, low, top_value):
    def one(dim, blocks):
        steps = jax.random.uniform(jax.random.fold_in(jax.random.fold_in(key, 6), dim), (blocks,), jnp.float32, low / len(cuts), top_value / len(cuts))
        return jnp.repeat(jnp.exp(steps), dims[dim] // blocks).reshape((-1,) + (1,) * (len(dims) - dim - 1))

    level = one(*cuts[0])
    for cut in cuts[1:]:
        level = level * one(*cut)
    return level


def gaussian(rng, extent, scale, limit, shards=(), held_as=jnp.bfloat16):
    loudness = block_scale(rng, extent, shards, -0.22, 0.18) if shards else 1.0
    entries = jax.random.normal(rng, extent, jnp.float32) * scale * loudness
    return jnp.minimum(jnp.maximum(entries, -limit), limit).astype(held_as)


def setup_inputs(seed: int = 0) -> dict:
    arg_keys = jax.random.split(jax.random.key(seed), 16)
    return {
        "tokens": gaussian(arg_keys[0], (TOKENS, MODEL_WIDTH), 1.0, 6.0, ((0, 8), (1, 4))),
        "norm_gain": jnp.clip(1.0 + 0.18 * jax.random.normal(arg_keys[1], (MODEL_WIDTH,), jnp.float32), 0.099609375, 1.8984375).astype(jnp.bfloat16),
        "w_query": gaussian(arg_keys[2], (MODEL_WIDTH, QUERY_HEADS * HEAD_SIZE), MODEL_WIDTH ** -0.5, 0.1875, ((0, 2), (1, 4))),
        "key_projection": gaussian(arg_keys[3], (MODEL_WIDTH, KEY_VALUE_HEADS * HEAD_SIZE), MODEL_WIDTH ** -0.5, 0.1875, ((0, 2), (1, 4))),
        "value_projection": gaussian(arg_keys[4], (MODEL_WIDTH, KEY_VALUE_HEADS * HEAD_SIZE), MODEL_WIDTH ** -0.5, 0.1875, ((0, 2), (1, 4))),
        "query_gain": jnp.clip(1.0 + 0.18 * jax.random.normal(arg_keys[5], (HEAD_SIZE,), jnp.float32), 0.099609375, 1.8984375).astype(jnp.bfloat16),
        "key_gain": jnp.clip(1.0 + 0.18 * jax.random.normal(arg_keys[6], (HEAD_SIZE,), jnp.float32), 0.099609375, 1.8984375).astype(jnp.bfloat16),
        "w_out": gaussian(arg_keys[7], (QUERY_HEADS * HEAD_SIZE, MODEL_WIDTH), (QUERY_HEADS * HEAD_SIZE // 16) ** -0.5, 0.5, ((0, 4), (1, 2))),
        "ffn_gain": jnp.clip(1.0 + 0.18 * jax.random.normal(arg_keys[8], (MODEL_WIDTH,), jnp.float32), 0.099609375, 1.8984375).astype(jnp.bfloat16),
        "w_gate": gaussian(arg_keys[9], (MODEL_WIDTH, FF), MODEL_WIDTH ** -0.5, 0.1875, ((0, 2), (1, 4))),
        "w_up": gaussian(arg_keys[10], (MODEL_WIDTH, FF), MODEL_WIDTH ** -0.5, 0.1875, ((0, 2), (1, 4))),
        "w_down": gaussian(arg_keys[11], (FF, MODEL_WIDTH), FF ** -0.5, 0.109375, ((0, 4), (1, 2))),
        "cotangent": gaussian(arg_keys[12], (TOKENS, MODEL_WIDTH), 1.0, 6.0, ((0, 8), (1, 4))),
        "sequence": draw_sequence(jax.random.fold_in(arg_keys[15], 71), 0),
        "position": draw_position(jax.random.fold_in(arg_keys[15], 71), 0),
    }


EPS = 1e-06
THETA = 1000000.0
HIGH = lax.Precision.HIGHEST

@jax.custom_vjp
def reduced_precision(v):
    return lax.optimization_barrier(v.astype(jnp.bfloat16)).astype(jnp.float32)

@jax.custom_vjp
def reduced_backward(v):
    return v

def low_keep(v):
    return (reduced_precision(v), None)

def low_pass(kept, grad):
    return (grad,)

def back_keep(v):
    return (v, None)

def back_low(kept, grad):
    return (reduced_precision(grad),)
reduced_precision.defvjp(low_keep, low_pass)
reduced_backward.defvjp(back_keep, back_low)

def matrix_product(left, right):
    return jnp.dot(left, right, precision=HIGH)

def head_norm(value_vectors, gain):
    return value_vectors * lax.rsqrt(lax.optimization_barrier(jnp.mean(value_vectors * value_vectors, axis=-1, keepdims=True)) + EPS) * gain

def rotate(value_vectors, cosine, sine):
    half = value_vectors.shape[-1] // 2
    turned = jnp.concatenate([-value_vectors[..., half:], value_vectors[..., :half]], axis=-1)
    return value_vectors * cosine + turned * sine

def angles(position, size):
    rates = THETA ** (-(jnp.arange(size // 2, dtype=jnp.float32) * 2.0) / size)
    phase = position.astype(jnp.float32)[:, None] * rates[None, :]
    phase = jnp.concatenate([phase, phase], axis=-1)
    return (jnp.cos(phase)[:, None, :], jnp.sin(phase)[:, None, :])

def attend(queries, key_vectors, value_vectors, sequence, position):
    query_group_ratio = QUERY_HEADS // KEY_VALUE_HEADS
    keys_wide = jnp.repeat(key_vectors, query_group_ratio, axis=1)
    values_wide = jnp.repeat(value_vectors, query_group_ratio, axis=1)
    token_length = queries.shape[0]
    block = min(512, token_length)
    count = token_length // block
    factor = HEAD_SIZE ** (-0.5)

    def one_block(block_data):
        query_block, seq_block, pos_block = block_data
        raw = jnp.einsum('qhd,khd->hqk', query_block, keys_wide, precision=HIGH)
        scores = reduced_backward(raw * factor)
        visible = (seq_block[:, None] == sequence[None, :]) & (position[None, :] <= pos_block[:, None])
        scores = jnp.where(visible[None], scores, -1e+30)
        probs = reduced_precision(jax.nn.softmax(scores, axis=-1))
        return jnp.einsum('hqk,khd->qhd', probs, values_wide, precision=HIGH)
    result = lax.map(jax.checkpoint(one_block), (queries.reshape(count, block, QUERY_HEADS, HEAD_SIZE), sequence.reshape(count, block), position.reshape(count, block)))
    return result.reshape(token_length, QUERY_HEADS * HEAD_SIZE)

def layer(inputs, gain_one, query_weight, key_matrix, value_matrix, query_scale, key_scale, out_weight, gain_two, gate_weight, up_weight, down_weight, sequence, position):
    token_length = inputs.shape[0]
    cosine, sine = angles(position, HEAD_SIZE)
    scale_one = lax.rsqrt(lax.optimization_barrier(jnp.mean(inputs * inputs, axis=-1, keepdims=True)) + EPS)
    normalized_rows = reduced_precision(inputs * scale_one * gain_one)
    queries = reduced_backward(matrix_product(normalized_rows, query_weight)).reshape(token_length, QUERY_HEADS, HEAD_SIZE)
    key_vectors = reduced_backward(matrix_product(normalized_rows, key_matrix)).reshape(token_length, KEY_VALUE_HEADS, HEAD_SIZE)
    value_vectors = reduced_precision(reduced_backward(matrix_product(normalized_rows, value_matrix))).reshape(token_length, KEY_VALUE_HEADS, HEAD_SIZE)
    queries = reduced_precision(rotate(head_norm(queries, query_scale), cosine, sine))
    key_vectors = reduced_precision(rotate(head_norm(key_vectors, key_scale), cosine, sine))
    mixed = reduced_precision(reduced_backward(attend(queries, key_vectors, value_vectors, sequence, position)))
    hidden = inputs + reduced_backward(matrix_product(mixed, out_weight))
    scale_two = lax.rsqrt(lax.optimization_barrier(jnp.mean(hidden * hidden, axis=-1, keepdims=True)) + EPS)
    normed_two = reduced_precision(hidden * scale_two * gain_two)
    gate = reduced_backward(matrix_product(normed_two, gate_weight))
    up = reduced_backward(matrix_product(normed_two, up_weight))
    product = reduced_precision(jax.nn.silu(gate) * up)
    return hidden + reduced_backward(matrix_product(product, down_weight))

def reference(tokens, norm_gain, w_query, key_projection, value_projection, query_gain, key_gain, w_out, ffn_gain, w_gate, w_up, w_down, cotangent, sequence, position):
    params = tuple((value.astype(jnp.float32) for value in (norm_gain, w_query, key_projection, value_projection, query_gain, key_gain, w_out, ffn_gain, w_gate, w_up, w_down)))
    blocks = tokens.shape[0] // GROUP

    def one_group(totals, block_data):
        block_tokens, block_cotangent, block_sequence, block_position = block_data

        def forward(block_input, *weights):
            return layer(block_input, *weights, block_sequence, block_position)
        result, backward = jax.vjp(forward, block_tokens.astype(jnp.float32), *params)
        grads = backward(block_cotangent.astype(jnp.float32))
        totals = tuple((carry + grad for carry, grad in zip(totals, grads[1:])))
        return (totals, (result.astype(jnp.bfloat16), grads[0]))
    zeros = tuple((jnp.zeros_like(value) for value in params))
    totals, (output, grad_tokens) = lax.scan(one_group, zeros, (tokens.reshape(blocks, GROUP, MODEL_WIDTH), cotangent.reshape(blocks, GROUP, MODEL_WIDTH), sequence.reshape(blocks, GROUP), position.reshape(blocks, GROUP)))
    return (output.reshape(blocks * GROUP, MODEL_WIDTH), grad_tokens.reshape(blocks * GROUP, MODEL_WIDTH), totals[0], totals[1], totals[2], totals[3], totals[4], totals[5], totals[6], totals[7], totals[8], totals[9], totals[10])
```

```python
import functools

import jax
import jax.numpy as jnp
from jax import lax
from jax.experimental import pallas as pl
from jax.experimental.pallas import tpu as pltpu
from jax.sharding import PartitionSpec as P

EPS = 1e-06
THETA = 1000000.0
NEGATIVE = -1e30
BF = jnp.bfloat16
F32 = jnp.float32
VMEM = pl.BlockSpec(memory_space=pltpu.VMEM)
SMEM = pl.BlockSpec(memory_space=pltpu.SMEM)


def dot(left, right):
    return lax.dot_general(left, right, (((1,), (0,)), ((), ())), preferred_element_type=F32)


def dot_cols(left, right):
    return lax.dot_general(left, right, (((1,), (1,)), ((), ())), preferred_element_type=F32)


def dot_rows(left, right):
    return lax.dot_general(left, right, (((0,), (0,)), ((), ())), preferred_element_type=F32)


def span(offset, size):
    return pl.ds(pl.multiple_of(offset, size), size)


def turn(vectors):
    return pltpu.roll(vectors, vectors.shape[-1] // 2, 1)


def shifted(block, axis, shift):
    size = lax.axis_size(axis)
    return lax.ppermute(block, axis, [(i, (i + shift) % size) for i in range(size)])


def pieces_of(block):
    return [block] + [shifted(block, "gx", s) for s in range(1, lax.axis_size("gx"))]


def piece_sum(own, others):
    total = own
    for s, part in enumerate(others, 1):
        total = total + shifted(part, "gx", s).astype(F32)
    return total


def gather_width(block, axis):
    if lax.axis_size("gy") == 2:
        return jnp.concatenate([block, shifted(block, "gy", 1)], axis=axis)
    return lax.all_gather(block, "gy", axis=axis, tiled=True)


def scatter_width(make, axis, width):
    count = lax.axis_size("gy")
    if count == 2:
        half = width // 2
        sent = make(half, half).astype(BF)
        return make(0, half) + shifted(sent, "gy", 1).astype(F32)
    return lax.psum_scatter(
        make(0, width).astype(BF), "gy", scatter_dimension=axis, tiled=True
    ).astype(F32)


def dev_sum(arrays):
    count = lax.axis_size("dev")
    here = lax.axis_index("dev")
    if count == 1:
        return arrays
    even = count & (count - 1) == 0

    def partner(m):
        return here ^ m if even else (here + m) % count

    def giver(m):
        return here ^ m if even else (here - m) % count

    def send(block, m):
        return lax.ppermute(
            block, "dev", [(i, i ^ m if even else (i + m) % count) for i in range(count)]
        )

    sizes = [a.shape[0] // count for a in arrays]
    low = [a.astype(BF) for a in arrays]
    mine = [
        lax.dynamic_slice_in_dim(a, here * size, size).astype(F32)
        for a, size in zip(arrays, sizes)
    ]
    for m in range(1, count):
        for k, (a, size) in enumerate(zip(low, sizes)):
            got = send(lax.dynamic_slice_in_dim(a, partner(m) * size, size), m)
            mine[k] = mine[k] + got.astype(F32)
    out = []
    for total, size, a in zip(mine, sizes, arrays):
        whole = jnp.zeros(a.shape, F32)
        whole = lax.dynamic_update_slice_in_dim(whole, total, here * size, 0)
        total = total.astype(BF)
        for m in range(1, count):
            whole = lax.dynamic_update_slice_in_dim(
                whole, send(total, m).astype(F32), giver(m) * size, 0
            )
        out.append(whole)
    return out


def small_sum(block, axis):
    total = block
    for s in range(1, lax.axis_size(axis)):
        total = total + shifted(block, axis, s)
    return total


def place(count, offset_ref, s):
    return lambda width: span(offset_ref[s], width)


def cot_kernel(count, offset_ref, *refs):
    pieces, (down_ref, whole_ref, grad_ref) = refs[:count], refs[count:]
    width = pieces[0].shape[1]
    for s in range(count):
        whole_ref[:, span(offset_ref[s], width)] = pieces[s][...]
    grad_ref[...] = dot_cols(whole_ref[...], down_ref[...])


def qkv_kernel(count, head, offset_ref, *refs):
    pieces = refs[:count]
    gain_ref, wq_ref, wk_ref, wv_ref, qg_ref, kg_ref, cos_ref, sin_ref = refs[count : count + 8]
    normed_ref, scale_ref, ql_ref, kl_ref, q_ref, k_ref, v_ref = refs[count + 8 :]
    width = pieces[0].shape[1]
    blocks = [p[...].astype(F32) for p in pieces]
    square = sum(jnp.sum(b * b, axis=1, keepdims=True) for b in blocks)
    scale = lax.rsqrt(square / (width * count) + EPS)
    scale_ref[...] = scale
    for s in range(count):
        normed_ref[:, span(offset_ref[s], width)] = (
            blocks[s] * scale * gain_ref[s : s + 1, :]
        ).astype(BF)
    normed = normed_ref[...]
    ql_ref[...] = dot(normed, wq_ref[...])
    kl_ref[...] = dot(normed, wk_ref[...])
    v_ref[...] = dot(normed, wv_ref[...]).astype(BF)
    cosine, sine = cos_ref[...], sin_ref[...]
    for lin_ref, gain, out_ref in ((ql_ref, qg_ref, q_ref), (kl_ref, kg_ref, k_ref)):
        for h in range(lin_ref.shape[1] // head):
            cut = slice(h * head, (h + 1) * head)
            u = lin_ref[:, cut]
            u = u * lax.rsqrt(jnp.mean(u * u, axis=1, keepdims=True) + EPS) * gain[...]
            out_ref[:, cut] = (u * cosine + turn(u) * sine).astype(BF)


def visible_bias(seq_col, pos_col, seq_row, pos_row):
    seen = (seq_col == seq_row) & (pos_col <= pos_row)
    return jnp.where(seen, 0.0, NEGATIVE)


def attend_kernel(
    head, tile, offset_ref, q_ref, k_ref, v_ref, row_ref, col_ref, wo_ref, *outs
):
    parts, (mixed_ref, att_ref, log_ref) = outs[:-3], outs[-3:]
    peers, rows = k_ref.shape[0], q_ref.shape[0]
    kv_heads = k_ref.shape[2] // head
    ratio = q_ref.shape[1] // head // kv_heads
    factor = head ** (-0.5)
    width = wo_ref.shape[1] // len(parts)
    for t in range(rows // tile):
        part = slice(t * tile, (t + 1) * tile)
        extent = (t + 1) * tile
        seq_row, pos_row = row_ref[0:1, part], row_ref[1:2, part]

        def bias_of(p):
            one = visible_bias(
                col_ref[p, :extent, 0:1], col_ref[p, :extent, 1:2], seq_row, pos_row
            )
            return jnp.concatenate([one] * ratio, axis=1)

        biases = [bias_of(p) for p in range(peers)] if peers <= 2 else None
        for j in range(kv_heads):
            cut = slice(j * head, (j + 1) * head)
            queries = jnp.concatenate(
                [
                    q_ref[part, (j * ratio + i) * head : (j * ratio + i + 1) * head]
                    for i in range(ratio)
                ],
                axis=0,
            )

            def step(p, carry, bias=None):
                high, total, accum = carry
                if bias is None:
                    bias = bias_of(p)
                scores = dot_cols(k_ref[p, :extent, cut], queries) * factor + bias
                newest = jnp.maximum(high, jnp.max(scores, axis=0, keepdims=True))
                weights = jnp.exp(scores - newest)
                shrink = jnp.exp(high - newest)
                total = total * shrink + jnp.sum(weights, axis=0, keepdims=True)
                accum = accum * shrink + dot_rows(v_ref[p, :extent, cut], weights.astype(BF))
                return newest, total, accum

            carry = (
                jnp.full((1, ratio * tile), NEGATIVE, F32),
                jnp.zeros((1, ratio * tile), F32),
                jnp.zeros((head, ratio * tile), F32),
            )
            if peers <= 2:
                for p in range(peers):
                    carry = step(p, carry, biases[p])
            else:
                carry = lax.fori_loop(0, peers, step, carry)
            high, total, accum = carry
            attended = accum / total
            logs = high + jnp.log(total)
            back = jnp.transpose(attended)
            for i in range(ratio):
                h = j * ratio + i
                lane = slice(i * tile, (i + 1) * tile)
                att_ref[h * head : (h + 1) * head, part] = attended[:, lane]
                log_ref[h : h + 1, part] = logs[:, lane]
                mixed_ref[part, h * head : (h + 1) * head] = back[lane, :].astype(BF)
    for s in range(len(parts)):
        weight = wo_ref[:, span(offset_ref[len(parts) + s], width)]
        parts[s][...] = dot(mixed_ref[...], weight).astype(parts[s].dtype)


def ffn_kernel(count, offset_ref, *refs):
    pieces = refs[:count]
    gain_ref, wg_ref, wu_ref, grad_ref = refs[count : count + 4]
    outs = refs[count + 4 :]
    parts, (normed_ref, scale_ref, product_ref, gate_ref, up_ref) = outs[:count], outs[count:]
    width = pieces[0].shape[1]
    blocks = [p[...].astype(F32) for p in pieces]
    square = sum(jnp.sum(b * b, axis=1, keepdims=True) for b in blocks)
    scale = lax.rsqrt(square / (width * count) + EPS)
    scale_ref[...] = scale
    for s in range(count):
        normed_ref[:, span(offset_ref[s], width)] = (
            blocks[s] * scale * gain_ref[s : s + 1, :]
        ).astype(BF)
    normed = normed_ref[...]
    gate = dot(normed, wg_ref[...])
    up = dot(normed, wu_ref[...])
    sig = 1.0 / (1.0 + jnp.exp(-gate))
    silu = gate * sig
    product_ref[...] = (silu * up).astype(BF)
    grad = grad_ref[...]
    gate_ref[...] = (grad * up * (sig + silu * (1.0 - sig))).astype(BF)
    up_ref[...] = (grad * silu).astype(BF)
    for s in range(count):
        at = span(offset_ref[count + s], width)
        parts[s][...] = (
            dot_cols(gate_ref[...], wg_ref[at, :]) + dot_cols(up_ref[...], wu_ref[at, :])
        ).astype(parts[s].dtype)


def split_dot_kernel(count, offset_ref, left_ref, weight_ref, *parts):
    width = weight_ref.shape[1] // count
    for s in range(count):
        weight = weight_ref[:, span(offset_ref[count + s], width)]
        parts[s][...] = dot(left_ref[...], weight).astype(parts[s].dtype)


def unrotate(grad, lin, gain, cosine, sine):
    size = lin.shape[1]
    inner = grad * cosine + turn(grad * sine)
    inverse = lax.rsqrt(jnp.mean(lin * lin, axis=1, keepdims=True) + EPS)
    unit = lin * inverse
    part = jnp.sum(inner * unit, axis=0, keepdims=True)
    inner = inner * gain
    mean = jnp.sum(inner * unit, axis=1, keepdims=True) / size
    return inverse * (inner - unit * mean), part


def attend_back_kernel(
    count, head, tile, offset_ref, *refs
):
    hidden, grads = refs[:count], refs[count : 2 * count]
    (gain_ref, scale_ref, cot_ref, wo_ref, q_ref, ql_ref, k_ref, v_ref, row_ref, col_ref,
     att_ref, log_ref, qg_ref, cos_ref, sin_ref) = refs[2 * count : 2 * count + 15]
    branch_ref, dql_ref, dk_ref, dv_ref, qpart_ref, dk_sum, dv_sum = refs[2 * count + 15 :]
    peers, rows = k_ref.shape[0], q_ref.shape[0]
    kv_heads = k_ref.shape[2] // head
    ratio = q_ref.shape[1] // head // kv_heads
    factor = head ** (-0.5)
    width = hidden[0].shape[1]
    dk_sum[...] = jnp.zeros_like(dk_sum)
    dv_sum[...] = jnp.zeros_like(dv_sum)
    gain_part = jnp.zeros((1, head), F32)
    for t in range(rows // tile):
        part = slice(t * tile, (t + 1) * tile)
        extent = (t + 1) * tile
        scale = scale_ref[part, :]
        blocks = [(h[part, :].astype(F32), g[part, :].astype(F32)) for h, g in zip(hidden, grads)]
        scaled = [g * gain_ref[s : s + 1, :] for s, (_, g) in enumerate(blocks)]
        inner = sum(
            jnp.sum(h * g, axis=1, keepdims=True) for (h, _), g in zip(blocks, scaled)
        )
        lessen = scale * scale * scale * (inner / (width * count))
        for s in range(count):
            at = span(offset_ref[s], width)
            branch_ref[part, at] = (
                cot_ref[part, at].astype(F32) + scale * scaled[s] - blocks[s][0] * lessen
            ).astype(BF)
        grad_mixed = dot_cols(branch_ref[part, :], wo_ref[...]).astype(BF)
        grad_back = jnp.transpose(grad_mixed.astype(F32))
        seq_row, pos_row = row_ref[0:1, part], row_ref[1:2, part]

        def bias_of(p):
            one = visible_bias(
                col_ref[p, :extent, 0:1], col_ref[p, :extent, 1:2], seq_row, pos_row
            )
            return jnp.concatenate([one] * ratio, axis=1)

        biases = [bias_of(p) for p in range(peers)] if peers <= 2 else None
        for j in range(kv_heads):
            cut = slice(j * head, (j + 1) * head)
            heads = [j * ratio + i for i in range(ratio)]
            lanes = [slice(h * head, (h + 1) * head) for h in heads]
            queries = jnp.concatenate([q_ref[part, lane] for lane in lanes], axis=0)
            grad_heads = jnp.concatenate([grad_mixed[:, lane] for lane in lanes], axis=0)
            logs = jnp.concatenate([log_ref[h : h + 1, part] for h in heads], axis=1)
            delta = jnp.concatenate(
                [
                    jnp.sum(grad_back[lane, :] * att_ref[lane, part], axis=0, keepdims=True)
                    for lane in lanes
                ],
                axis=1,
            )

            def step(p, accum, bias=None):
                if bias is None:
                    bias = bias_of(p)
                keys, values = k_ref[p, :extent, cut], v_ref[p, :extent, cut]
                probs = jnp.exp(dot_cols(keys, queries) * factor + bias - logs)
                grad_probs = dot_cols(values, grad_heads)
                grad_scores = (probs * (grad_probs - delta)).astype(BF)
                dv_sum[p, :extent, cut] += dot(probs.astype(BF), grad_heads)
                dk_sum[p, :extent, cut] += dot(grad_scores, queries)
                return accum + dot_rows(keys, grad_scores)

            accum = jnp.zeros((head, ratio * tile), F32)
            if peers <= 2:
                for p in range(peers):
                    accum = step(p, accum, biases[p])
            else:
                accum = lax.fori_loop(0, peers, step, accum)
            grad_query = jnp.transpose(accum) * factor
            for i, lane in enumerate(lanes):
                lin, one = unrotate(
                    grad_query[i * tile : (i + 1) * tile, :],
                    ql_ref[part, lane],
                    qg_ref[...],
                    cos_ref[part, :],
                    sin_ref[part, :],
                )
                dql_ref[part, lane] = lin.astype(BF)
                gain_part = gain_part + one
    qpart_ref[...] = gain_part
    dk_ref[...] = (dk_sum[...] * factor).astype(dk_ref.dtype)
    dv_ref[...] = dv_sum[...].astype(dv_ref.dtype)


def lin_back_kernel(count, head, parts_in, offset_ref, *refs):
    (dql_ref, ql_ref, kl_ref, v_ref) = refs[:4]
    dks, dvs = refs[4 : 4 + parts_in], refs[4 + parts_in : 4 + 2 * parts_in]
    (kg_ref, cos_ref, sin_ref, wq_ref, wk_ref, wv_ref, normed_ref) = refs[
        4 + 2 * parts_in : 11 + 2 * parts_in
    ]
    outs = refs[11 + 2 * parts_in :]
    parts, (dkl_ref, dvl_ref, inner_ref, kpart_ref, npart_ref) = outs[:count], outs[count:]
    width = wq_ref.shape[0] // count

    @pl.when(pl.program_id(0) == 0)
    def _():
        kpart_ref[...] = jnp.zeros_like(kpart_ref)
        npart_ref[...] = jnp.zeros_like(npart_ref)

    grad_keys = sum(r[...].astype(F32) for r in dks)
    dvl_ref[...] = sum(r[...].astype(F32) for r in dvs).astype(BF)
    for h in range(kl_ref.shape[1] // head):
        cut = slice(h * head, (h + 1) * head)
        lin, one = unrotate(
            grad_keys[:, cut], kl_ref[:, cut], kg_ref[...], cos_ref[...], sin_ref[...]
        )
        dkl_ref[:, cut] = lin.astype(BF)
        kpart_ref[...] += one
    grad_q, grad_k, grad_v = dql_ref[...], dkl_ref[...], dvl_ref[...]
    inner_ref[...] = (
        jnp.sum(grad_q.astype(F32) * ql_ref[...], axis=1, keepdims=True)
        + jnp.sum(grad_k.astype(F32) * kl_ref[...], axis=1, keepdims=True)
        + jnp.sum(grad_v.astype(F32) * v_ref[...].astype(F32), axis=1, keepdims=True)
    )
    for s in range(count):
        at = span(offset_ref[count + s], width)
        term = (
            dot_cols(grad_q, wq_ref[at, :])
            + dot_cols(grad_k, wk_ref[at, :])
            + dot_cols(grad_v, wv_ref[at, :])
        )
        parts[s][...] = term.astype(parts[s].dtype)


def out(shape, dtype):
    return jax.ShapeDtypeStruct(shape, dtype)


def rows_block(tile, width):
    return pl.BlockSpec((tile, width), lambda i: (i, 0))


def same_block(shape):
    return pl.BlockSpec(shape, lambda i: (0,) * len(shape))


def call(kernel, grid, in_specs, out_specs, out_shape, flops, scratch=()):
    extra = dict(grid=grid) if grid else {}
    return pl.pallas_call(
        kernel,
        in_specs=in_specs,
        out_specs=out_specs,
        out_shape=out_shape,
        scratch_shapes=scratch,
        compiler_params=pltpu.CompilerParams(vmem_limit_bytes=50 * 2**20),
        cost_estimate=pl.CostEstimate(
            flops=flops, bytes_accessed=4 * 2**20, transcendentals=0
        ),
        **extra,
    )


def per_device(
    tokens,
    norm_gain,
    w_query,
    key_projection,
    value_projection,
    query_gain,
    key_gain,
    w_out,
    ffn_gain,
    w_gate,
    w_up,
    w_down,
    cotangent,
    sequence,
    position,
):
    rows, piece = tokens.shape
    count = lax.axis_size("gx")
    peers = lax.axis_size("gy")
    width = piece * count
    head = query_gain.shape[0]
    q_cols, kv_cols, hidden_units = w_query.shape[1], key_projection.shape[1], w_gate.shape[1]
    gx, gy = lax.axis_index("gx"), lax.axis_index("gy")
    tile = min(256, rows)
    small_tile = min(128, rows)
    grid = (rows // tile,)

    def lies_at(block):
        if peers == 2 and count % 2 == 0:
            half = count // 2
            return ((block // half) ^ gy) * (half * piece) + (block % half) * piece
        return block * piece

    offsets = jnp.stack(
        [lies_at((gx - s) % count) for s in range(count)]
        + [lies_at((gx + s) % count) for s in range(count)]
    ).astype(jnp.int32)

    gains = jnp.stack([norm_gain, ffn_gain] + [norm_gain] * 14).astype(F32)[:8]
    token_pieces = pieces_of(tokens)
    gain_pieces = pieces_of(gains)
    gain_one = jnp.concatenate([g[0:1] for g in gain_pieces], axis=0)
    gain_two = jnp.concatenate([g[1:2] for g in gain_pieces], axis=0)
    full_query, full_key, full_value = (
        gather_width(w, 0) for w in (w_query, key_projection, value_projection)
    )
    full_out = gather_width(w_out, 1)
    full_down = gather_width(w_down, 1)
    full_gate, full_up = gather_width(w_gate, 0), gather_width(w_up, 0)
    cot_pieces = pieces_of(cotangent)

    all_seq, all_pos = sequence.reshape(peers, rows), position.reshape(peers, rows)
    if peers == 2:
        order = lambda a: jnp.where(gy == 0, a, a[::-1])
        all_seq, all_pos = order(all_seq), order(all_pos)
        own_seq, own_pos = all_seq[0], all_pos[0]
    else:
        own_seq = lax.dynamic_index_in_dim(all_seq, gy, 0, False)
        own_pos = lax.dynamic_index_in_dim(all_pos, gy, 0, False)
    row_info = jnp.concatenate(
        [own_seq[None], own_pos[None], jnp.zeros((6, rows), jnp.int32)], axis=0
    )
    col_info = jnp.stack([all_seq, all_pos], axis=-1)
    rates = THETA ** (-(jnp.arange(head // 2, dtype=F32) * 2.0) / head)
    phase = own_pos.astype(F32)[:, None] * rates[None, :]
    cosine = jnp.concatenate([jnp.cos(phase)] * 2, axis=1)
    sine = jnp.concatenate([-jnp.sin(phase), jnp.sin(phase)], axis=1)
    q_scale = query_gain.astype(F32)[None]
    k_scale = key_gain.astype(F32)[None]

    normed_one, scale_one, query_lin, key_lin, query_bf, key_bf, value_bf = call(
        functools.partial(qkv_kernel, count, head),
        grid,
        [SMEM]
        + [rows_block(tile, piece)] * count
        + [
            same_block((count, piece)),
            same_block((width, q_cols)),
            same_block((width, kv_cols)),
            same_block((width, kv_cols)),
            same_block((1, head)),
            same_block((1, head)),
            rows_block(tile, head),
            rows_block(tile, head),
        ],
        [
            rows_block(tile, width),
            rows_block(tile, 1),
            rows_block(tile, q_cols),
            rows_block(tile, kv_cols),
            rows_block(tile, q_cols),
            rows_block(tile, kv_cols),
            rows_block(tile, kv_cols),
        ],
        [
            out((rows, width), BF),
            out((rows, 1), F32),
            out((rows, q_cols), F32),
            out((rows, kv_cols), F32),
            out((rows, q_cols), BF),
            out((rows, kv_cols), BF),
            out((rows, kv_cols), BF),
        ],
        2 * rows * width * (q_cols + 2 * kv_cols),
    )(
        offsets, *token_pieces, gain_one, full_query, full_key, full_value,
        q_scale, k_scale, cosine, sine,
    )

    if peers == 2:
        all_keys = jnp.stack([key_bf, shifted(key_bf, "gy", 1)])
        all_values = jnp.stack([value_bf, shifted(value_bf, "gy", 1)])
    else:
        all_keys = lax.all_gather(key_bf, "gy", axis=0)
        all_values = lax.all_gather(value_bf, "gy", axis=0)

    split_out = [out((rows, piece), F32)] + [out((rows, piece), BF)] * (count - 1)
    attend_flops = 4 * rows * rows * peers * q_cols
    *out_parts, mixed, attended, logs = call(
        functools.partial(attend_kernel, head, small_tile),
        None,
        [SMEM] + [VMEM] * 6,
        [VMEM] * (count + 3),
        split_out
        + [
            out((rows, q_cols), BF),
            out((q_cols, rows), F32),
            out((max(8, q_cols // head), rows), F32),
        ],
        attend_flops + 2 * rows * q_cols * width,
    )(offsets, query_bf, all_keys, all_values, row_info, col_info, full_out)

    cot_whole, grad_product = call(
        functools.partial(cot_kernel, count),
        grid,
        [SMEM] + [rows_block(tile, piece)] * count + [same_block((hidden_units, width))],
        [rows_block(tile, width), rows_block(tile, hidden_units)],
        [out((rows, width), BF), out((rows, hidden_units), F32)],
        2 * rows * width * hidden_units,
    )(offsets, *cot_pieces, full_down)

    inputs = tokens.astype(F32)
    hidden = inputs + piece_sum(out_parts[0], out_parts[1:])
    hidden_pieces = pieces_of(hidden.astype(BF))

    *grad_parts, normed_two, scale_two, product, gate_bf, up_bf = call(
        functools.partial(ffn_kernel, count),
        grid,
        [SMEM]
        + [rows_block(tile, piece)] * count
        + [
            same_block((count, piece)),
            same_block((width, hidden_units)),
            same_block((width, hidden_units)),
            rows_block(tile, hidden_units),
        ],
        [rows_block(tile, piece)] * count
        + [
            rows_block(tile, width),
            rows_block(tile, 1),
            rows_block(tile, hidden_units),
            rows_block(tile, hidden_units),
            rows_block(tile, hidden_units),
        ],
        split_out
        + [
            out((rows, width), BF),
            out((rows, 1), F32),
            out((rows, hidden_units), BF),
            out((rows, hidden_units), BF),
            out((rows, hidden_units), BF),
        ],
        8 * rows * width * hidden_units,
    )(offsets, *hidden_pieces, gain_two, full_gate, full_up, grad_product)

    grad_normed_two = piece_sum(grad_parts[0], grad_parts[1:])
    grad_pieces = pieces_of(grad_normed_two.astype(BF))

    result_parts = call(
        functools.partial(split_dot_kernel, count),
        grid,
        [SMEM, rows_block(tile, hidden_units), same_block((hidden_units, width))],
        [rows_block(tile, piece)] * count,
        split_out,
        2 * rows * width * hidden_units,
    )(offsets, product, full_down)
    result = hidden + piece_sum(result_parts[0], result_parts[1:])

    def rows_share(whole, grads):
        return scatter_width(
            lambda start, size: dot_rows(whole[:, start : start + size], grads), 0, width
        )

    def cols_share(left, whole):
        return scatter_width(
            lambda start, size: dot_rows(left, whole[:, start : start + size]), 1, width
        )

    down_grad = cols_share(product, cot_whole)
    gate_grad = rows_share(normed_two, gate_bf)
    up_grad = rows_share(normed_two, up_bf)
    down_grad, gate_grad, up_grad = dev_sum([down_grad, gate_grad, up_grad])

    branch, grad_query_lin, key_parts, value_parts, query_gain_part = call(
        functools.partial(attend_back_kernel, count, head, small_tile),
        None,
        [SMEM] + [VMEM] * (2 * count + 15),
        [VMEM] * 5,
        [
            out((rows, width), BF),
            out((rows, q_cols), BF),
            out((peers, rows, kv_cols), BF),
            out((peers, rows, kv_cols), BF),
            out((1, head), F32),
        ],
        5 * attend_flops // 2 + 2 * rows * q_cols * width,
        [pltpu.VMEM((peers, rows, kv_cols), F32), pltpu.VMEM((peers, rows, kv_cols), F32)],
    )(
        offsets, *hidden_pieces, *grad_pieces, gain_two, scale_two, cot_whole, full_out,
        query_bf, query_lin, all_keys, all_values, row_info, col_info, attended, logs,
        q_scale, cosine, sine,
    )
    if peers == 2:
        key_terms = [key_parts[0], shifted(key_parts[1], "gy", 1)]
        value_terms = [value_parts[0], shifted(value_parts[1], "gy", 1)]
    else:
        share = lambda a: lax.psum_scatter(a, "gy", scatter_dimension=0, tiled=True)[0]
        key_terms, value_terms = [share(key_parts)], [share(value_parts)]

    out_grad = cols_share(mixed, branch)
    (out_grad,) = dev_sum([out_grad])

    *last_parts, grad_key_lin, grad_value_lin, inner_part, key_gain_part, _ = call(
        functools.partial(lin_back_kernel, count, head, len(key_terms)),
        grid,
        [SMEM]
        + [rows_block(tile, q_cols), rows_block(tile, q_cols), rows_block(tile, kv_cols)]
        + [rows_block(tile, kv_cols)] * (1 + 2 * len(key_terms))
        + [
            same_block((1, head)),
            rows_block(tile, head),
            rows_block(tile, head),
            same_block((width, q_cols)),
            same_block((width, kv_cols)),
            same_block((width, kv_cols)),
            rows_block(tile, width),
        ],
        [rows_block(tile, piece)] * count
        + [
            rows_block(tile, kv_cols),
            rows_block(tile, kv_cols),
            rows_block(tile, 1),
            same_block((1, head)),
            same_block((1, head)),
        ],
        split_out
        + [
            out((rows, kv_cols), BF),
            out((rows, kv_cols), BF),
            out((rows, 1), F32),
            out((1, head), F32),
            out((1, head), F32),
        ],
        2 * rows * width * (q_cols + 2 * kv_cols),
    )(
        offsets, grad_query_lin, query_lin, key_lin, value_bf, *key_terms, *value_terms,
        k_scale, cosine, sine, full_query, full_key, full_value, normed_one,
    )

    query_grad = rows_share(normed_one, grad_query_lin)
    key_grad = rows_share(normed_one, grad_key_lin)
    value_grad = rows_share(normed_one, grad_value_lin)
    query_grad, key_grad, value_grad = dev_sum([query_grad, key_grad, value_grad])

    pad = lambda a, n: jnp.pad(a, ((0, 0), (0, n - a.shape[1])))
    wide = max(rows, head)
    small = jnp.concatenate(
        [
            pad(inner_part.reshape(1, rows), wide),
            pad(query_gain_part, wide),
            pad(key_gain_part, wide),
            jnp.zeros((5, wide), F32),
        ],
        axis=0,
    )
    small = small_sum(small, "gx")
    inner_one = small[0, :rows][:, None] / scale_one

    grad_normed_one = piece_sum(last_parts[0], last_parts[1:])
    own_gain_one, own_gain_two = norm_gain.astype(F32), ffn_gain.astype(F32)
    scaled_two = grad_normed_two * own_gain_two
    inner_two = sum(
        jnp.sum(h.astype(F32) * g.astype(F32) * gain_two[s], axis=1, keepdims=True)
        for s, (h, g) in enumerate(zip(hidden_pieces, grad_pieces))
    )
    grad_hidden = (
        cotangent.astype(F32)
        + scale_two * scaled_two
        - hidden * scale_two**3 * (inner_two / width)
    )
    grad_inputs = (
        grad_hidden
        + scale_one * own_gain_one * grad_normed_one
        - inputs * scale_one**3 * (inner_one / width)
    )
    gain_two_part = jnp.sum(grad_normed_two * hidden * scale_two, axis=0)
    gain_one_part = jnp.sum(grad_normed_one * inputs * scale_one, axis=0)
    last = jnp.concatenate([gain_one_part, gain_two_part, small[1, :head], small[2, :head]])
    length = last.shape[0]
    last = jnp.pad(last, (0, -length % 1024)).reshape(8, -1)
    if peers == 2:
        last = small_sum(small_sum(last, "gy"), "dev")
    else:
        last = lax.psum(last, ("dev", "gy"))
    last = last.reshape(-1)
    return (
        result.astype(BF),
        grad_inputs,
        last[:piece],
        query_grad,
        key_grad,
        value_grad,
        last[2 * piece : 2 * piece + head],
        last[2 * piece + head : 2 * piece + 2 * head],
        out_grad,
        last[piece : 2 * piece],
        gate_grad,
        up_grad,
        down_grad,
    )


def solution(mesh):
    wide = P(("dev", "gy"), "gx")
    weight, back = P("gy", "gx"), P("gx", "gy")
    return jax.shard_map(
        per_device,
        mesh=mesh,
        in_specs=(
            wide, P("gx"), weight, weight, weight, P(), P(), back, P("gx"), weight, weight, back,
            wide, P("dev"), P("dev"),
        ),
        out_specs=(
            wide, wide, P("gx"), weight, weight, weight, P(), P(), back, P("gx"), weight, weight,
            back,
        ),
        check_vma=False,
    )
```

```python
import functools

import jax
import jax.numpy as jnp
from jax import lax
from jax.experimental import pallas as pl
from jax.experimental.pallas import tpu as pltpu
from jax.sharding import PartitionSpec as P

EPS = 1e-06
THETA = 1000000.0
NEGATIVE = -1e30
BF = jnp.bfloat16
F32 = jnp.float32
VMEM = pl.BlockSpec(memory_space=pltpu.VMEM)
SMEM = pl.BlockSpec(memory_space=pltpu.SMEM)
ANY = pl.BlockSpec(memory_space=pl.ANY)


def dot(left, right):
    return lax.dot_general(left, right, (((1,), (0,)), ((), ())), preferred_element_type=F32)


def dot_cols(left, right):
    return lax.dot_general(left, right, (((1,), (1,)), ((), ())), preferred_element_type=F32)


def dot_rows(left, right):
    return lax.dot_general(left, right, (((0,), (0,)), ((), ())), preferred_element_type=F32)


def span(offset, size):
    return pl.ds(pl.multiple_of(offset, size), size)


def turn(vectors):
    return pltpu.roll(vectors, vectors.shape[-1] // 2, 1)


def shifted(block, axis, shift):
    size = lax.axis_size(axis)
    return lax.ppermute(block, axis, [(i, (i + shift) % size) for i in range(size)])


def pieces_of(block):
    return [block] + [shifted(block, "gx", s) for s in range(1, lax.axis_size("gx"))]


def piece_sum(own, others):
    total = own
    for s, part in enumerate(others, 1):
        total = total + shifted(part, "gx", s).astype(F32)
    return total


def gather_width(block, axis):
    if lax.axis_size("gy") == 2:
        return [block, shifted(block, "gy", 1)]
    return [lax.all_gather(block, "gy", axis=axis, tiled=True)]


def dev_partner(m):
    count, here = lax.axis_size("dev"), lax.axis_index("dev")
    return here ^ m if count & (count - 1) == 0 else (here + m) % count


def dev_giver(m):
    count, here = lax.axis_size("dev"), lax.axis_index("dev")
    return here ^ m if count & (count - 1) == 0 else (here - m) % count


def dev_send(block, m):
    count = lax.axis_size("dev")
    even = count & (count - 1) == 0
    return lax.ppermute(
        block, "dev", [(i, i ^ m if even else (i + m) % count) for i in range(count)]
    )


def nothing(*refs):
    pass


def after(arrays, *deps):
    if not deps or not arrays:
        return arrays
    return pl.pallas_call(
        nothing,
        in_specs=[ANY] * (len(arrays) + len(deps)),
        out_specs=[ANY] * len(arrays),
        out_shape=[jax.ShapeDtypeStruct(a.shape, a.dtype) for a in arrays],
        input_output_aliases={i: i for i in range(len(arrays))},
    )(*arrays, *deps)


def small_sum(block, axis):
    total = block
    for s in range(1, lax.axis_size(axis)):
        total = total + shifted(block, axis, s)
    return total


def pick(refs, offset, size, axis):
    half = refs[0].shape[axis]

    def cut(ref):
        at = span(offset % half, size)
        return ref[at, :] if axis == 0 else ref[:, at]

    if len(refs) == 1:
        return cut(refs[0])
    return jnp.where(offset < half, cut(refs[0]), cut(refs[1]))


def wide_dot(left_ref, refs, product, axis):
    step = left_ref.shape[1] // len(refs)
    return sum(
        product(left_ref[:, i * step : (i + 1) * step], ref[...]) for i, ref in enumerate(refs)
    )


def normalise(pieces, gains, row, offset_ref, normed_ref, scale_ref):
    count, width = len(pieces), pieces[0].shape[1]
    blocks = [p[...].astype(F32) for p in pieces]
    square = sum(jnp.sum(b * b, axis=1, keepdims=True) for b in blocks)
    scale = lax.rsqrt(square / (width * count) + EPS)
    scale_ref[...] = scale
    for s in range(count):
        gain = gains[s][row : row + 1, :].astype(F32)
        normed_ref[:, span(offset_ref[s], width)] = (blocks[s] * scale * gain).astype(BF)


def cot_kernel(count, offset_ref, *refs):
    pieces, normed_ref, downs = refs[:count], refs[count], refs[count + 1 : -3]
    whole_ref, grad_ref, turned_ref = refs[-3:]
    turned_ref[...] = jnp.transpose(normed_ref[...])
    width = pieces[0].shape[1]
    for s in range(count):
        whole_ref[:, span(offset_ref[s], width)] = pieces[s][...]
    grad_ref[...] = wide_dot(whole_ref, downs, dot_cols, 1)


def qkv_kernel(count, parts, head, offset_ref, *refs):
    pieces, gains, refs = refs[:count], refs[count : 2 * count], refs[2 * count :]
    wq, wk, wv = refs[:parts], refs[parts : 2 * parts], refs[2 * parts : 3 * parts]
    qg_ref, kg_ref, cos_ref, sin_ref = refs[3 * parts : 3 * parts + 4]
    normed_ref, scale_ref, ql_ref, kl_ref, q_ref, k_ref, v_ref = refs[-7:]
    normalise(pieces, gains, 0, offset_ref, normed_ref, scale_ref)
    ql_ref[...] = wide_dot(normed_ref, wq, dot, 0)
    kl_ref[...] = wide_dot(normed_ref, wk, dot, 0)
    v_ref[...] = wide_dot(normed_ref, wv, dot, 0).astype(BF)
    cosine, sine = cos_ref[...], sin_ref[...]
    for lin_ref, gain, out_ref in ((ql_ref, qg_ref, q_ref), (kl_ref, kg_ref, k_ref)):
        for h in range(lin_ref.shape[1] // head):
            cut = slice(h * head, (h + 1) * head)
            u = lin_ref[:, cut]
            u = u * lax.rsqrt(jnp.mean(u * u, axis=1, keepdims=True) + EPS) * gain[...]
            out_ref[:, cut] = (u * cosine + turn(u) * sine).astype(BF)


def visible_bias(seq_col, pos_col, seq_row, pos_row):
    seen = (seq_col == seq_row) & (pos_col <= pos_row)
    return jnp.where(seen, 0.0, NEGATIVE)


def peer_block(refs, p, extent, cut):
    return refs[p][:extent, cut] if len(refs) > 1 else refs[0][p, :extent, cut]


def columns_of(col_ref, peers):
    if peers > 2:
        return lambda p, extent: (col_ref[p, :extent, 0:1], col_ref[p, :extent, 1:2])
    turned = jnp.transpose(col_ref[...])
    return lambda p, extent: (
        turned[:extent, 2 * p : 2 * p + 1],
        turned[:extent, 2 * p + 1 : 2 * p + 2],
    )


def attend_kernel(head, tile, peers, q_ref, row_ref, col_ref, *refs):
    each = peers if peers <= 2 else 1
    keys, values = refs[:each], refs[each : 2 * each]
    mixed_ref, att_ref, log_ref = refs[-3:]
    column = columns_of(col_ref, peers)
    rows = q_ref.shape[0]
    kv_heads = keys[0].shape[-1] // head
    ratio = q_ref.shape[1] // head // kv_heads
    factor = head ** (-0.5)
    for t in range(rows // tile):
        part = slice(t * tile, (t + 1) * tile)
        extent = (t + 1) * tile
        seq_row, pos_row = row_ref[0:1, part], row_ref[1:2, part]

        def bias_of(p):
            one = visible_bias(*column(p, extent), seq_row, pos_row)
            return jnp.concatenate([one] * ratio, axis=1)

        biases = [bias_of(p) for p in range(peers)] if peers <= 2 else None
        for j in range(kv_heads):
            cut = slice(j * head, (j + 1) * head)
            queries = jnp.concatenate(
                [
                    q_ref[part, (j * ratio + i) * head : (j * ratio + i + 1) * head]
                    for i in range(ratio)
                ],
                axis=0,
            )

            def step(p, carry, bias=None):
                high, total, accum = carry
                if bias is None:
                    bias = bias_of(p)
                scores = dot_cols(peer_block(keys, p, extent, cut), queries) * factor + bias
                newest = jnp.maximum(high, jnp.max(scores, axis=0, keepdims=True))
                weights = jnp.exp(scores - newest)
                shrink = jnp.exp(high - newest)
                total = total * shrink + jnp.sum(weights, axis=0, keepdims=True)
                accum = accum * shrink + dot_rows(
                    peer_block(values, p, extent, cut), weights.astype(BF)
                )
                return newest, total, accum

            carry = (
                jnp.full((1, ratio * tile), NEGATIVE, F32),
                jnp.zeros((1, ratio * tile), F32),
                jnp.zeros((head, ratio * tile), F32),
            )
            if peers <= 2:
                for p in range(peers):
                    carry = step(p, carry, biases[p])
            else:
                carry = lax.fori_loop(0, peers, step, carry)
            high, total, accum = carry
            attended = accum / total
            logs = high + jnp.log(total)
            back = jnp.transpose(attended)
            for i in range(ratio):
                h = j * ratio + i
                lane = slice(i * tile, (i + 1) * tile)
                att_ref[h * head : (h + 1) * head, part] = attended[:, lane]
                log_ref[h : h + 1, part] = logs[:, lane]
                mixed_ref[part, h * head : (h + 1) * head] = back[lane, :].astype(BF)


def ffn_kernel(count, parts_in, offset_ref, *refs):
    pieces, gains, refs = refs[:count], refs[count : 2 * count], refs[2 * count :]
    wg, wu, grad_ref = refs[:parts_in], refs[parts_in : 2 * parts_in], refs[2 * parts_in]
    outs = refs[-count - 5 :]
    parts, (normed_ref, scale_ref, product_ref, gate_ref, up_ref) = outs[:count], outs[count:]
    width = pieces[0].shape[1]
    normalise(pieces, gains, 1, offset_ref, normed_ref, scale_ref)
    gate = wide_dot(normed_ref, wg, dot, 0)
    up = wide_dot(normed_ref, wu, dot, 0)
    sig = 1.0 / (1.0 + jnp.exp(-gate))
    silu = gate * sig
    product_ref[...] = (silu * up).astype(BF)
    grad = grad_ref[...]
    gate_ref[...] = (grad * up * (sig + silu * (1.0 - sig))).astype(BF)
    up_ref[...] = (grad * silu).astype(BF)
    for s in range(count):
        at = offset_ref[count + s]
        parts[s][...] = (
            dot_cols(gate_ref[...], pick(wg, at, width, 0))
            + dot_cols(up_ref[...], pick(wu, at, width, 0))
        ).astype(parts[s].dtype)


def split_dot_kernel(count, parts_in, offset_ref, left_ref, *refs):
    weights, parts = refs[:parts_in], refs[-count:]
    width = parts[0].shape[1]
    for s in range(count):
        weight = pick(weights, offset_ref[count + s], width, 1)
        parts[s][...] = dot(left_ref[...], weight).astype(parts[s].dtype)


def weight_grad_kernel(turned, *refs):
    own_ref, other_ref = refs[-2:]
    size = own_ref.shape[1]
    start = 0
    for i, across in enumerate(turned):
        own, other, right = refs[3 * i : 3 * i + 3]
        width = right.shape[1]
        both = jnp.concatenate([own[...], other[...]], axis=0 if across else 1)
        both = (dot if across else dot_rows)(both, right[...])
        own_ref[0, :, start : start + width] = both[:size].astype(BF)
        other_ref[0, :, start : start + width] = both[size:].astype(BF)
        start += width


def final_kernel(count, *refs):
    parts = refs[:count]
    (tok_ref, cot_ref, hid_ref, two_ref, one_scale, two_scale, two_inner, gain_ref) = refs[
        count : count + 8
    ]
    grad_ref, part_ref = refs[-2:]
    rows, width = tok_ref.shape
    size = width * count
    gain_one, gain_two = gain_ref[0:1, :].astype(F32), gain_ref[1:2, :].astype(F32)
    sums = [jnp.zeros((1, width), F32)] * 2
    small = sum(p[rows : rows + 16, :].astype(F32) for p in parts)
    count_rows = rows // width
    for i in range(count_rows):
        at = slice(i * width, (i + 1) * width)
        one = sum(p[at, :].astype(F32) for p in parts)
        inputs, hidden, two = tok_ref[at, :].astype(F32), hid_ref[at, :], two_ref[at, :]
        scale, later = one_scale[at, :], two_scale[at, :]
        inner = small[i : i + 1, :] + small[count_rows + i : count_rows + i + 1, :]
        inner = jnp.transpose(jnp.broadcast_to(inner, (128, width)))[:, 0:1]
        grad_ref[at, :] = (
            cot_ref[at, :].astype(F32)
            + later * (two * gain_two)
            - hidden * (later * later * later * (two_inner[at, :] / size))
            + scale * (one * gain_one)
            - inputs * (scale * scale * (inner / size))
        )
        sums[0] = sums[0] + jnp.sum(one * inputs * scale, axis=0, keepdims=True)
        sums[1] = sums[1] + jnp.sum(two * hidden * later, axis=0, keepdims=True)
    last = 2 * count_rows
    part_ref[...] = jnp.concatenate(
        sums
        + [small[last : last + 1, :] + small[last + 1 : last + 2, :], jnp.zeros((5, width), F32)],
        axis=0,
    )


def share_sum_kernel(shares, chunk_ref, *refs):
    owns, gots = refs[:shares], refs[shares : 2 * shares]
    blocks = owns[0].shape[0]
    for m, ref in enumerate(refs[-blocks:]):
        c = chunk_ref[m]
        start = 0
        for own, got in zip(owns, gots):
            stop = start + own.shape[2]
            ref[:, start:stop] = (own[c].astype(F32) + got[c].astype(F32)).astype(ref.dtype)
            start = stop


def result_share_kernel(count, parts_in, offset_ref, left_ref, *refs):
    weights, (own_ref, got_ref) = refs[:parts_in], refs[parts_in : parts_in + 2]
    split_dot_kernel(count, parts_in, offset_ref, left_ref, *weights, *refs[-count - 1 : -1])
    refs[-1][...] = (own_ref[0].astype(F32) + got_ref[0].astype(F32)).astype(BF)


def widen_kernel(pieces, whole_ref, *refs):
    for (start, width, turned), ref in zip(pieces, refs[-len(pieces) :]):
        value = whole_ref[:, start : start + width].astype(F32)
        ref[...] = jnp.transpose(value) if turned else value


def assemble_kernel(count, pieces, owner_ref, *refs):
    parts, outs = refs[:count], refs[-len(pieces) - 1 : -1]
    held = refs[-1]
    size = parts[0].shape[0]
    for (start, width, turned), ref in zip(pieces, outs):
        for m, part in enumerate(parts):
            at = pl.ds(pl.multiple_of(owner_ref[m] * size, size), size)
            value = part[:, start : start + width].astype(F32)
            if turned:
                held[at, :width] = value
            else:
                ref[at, :] = value
        if turned:
            ref[...] = jnp.transpose(held[:, :width])


def unrotate(grad, lin, gain, cosine, sine):
    size = lin.shape[1]
    inner = grad * cosine + turn(grad * sine)
    inverse = lax.rsqrt(jnp.mean(lin * lin, axis=1, keepdims=True) + EPS)
    unit = lin * inverse
    part = jnp.sum(inner * unit, axis=0, keepdims=True)
    inner = inner * gain
    mean = jnp.sum(inner * unit, axis=1, keepdims=True) / size
    return inverse * (inner - unit * mean), part


def branch_kernel(count, parts_in, offset_ref, *refs):
    hidden, grads, gains = refs[:count], refs[count : 2 * count], refs[2 * count : 3 * count]
    scale_ref, cot_ref = refs[3 * count : 3 * count + 2]
    weights = refs[3 * count + 2 : 3 * count + 2 + parts_in]
    branch_ref, mixed_ref, inner_ref = refs[-3:]
    width = hidden[0].shape[1]
    scale = scale_ref[...]
    blocks = [(h[...].astype(F32), g[...].astype(F32)) for h, g in zip(hidden, grads)]
    scaled = [g * gain[1:2, :].astype(F32) for gain, (_, g) in zip(gains, blocks)]
    inner = sum(jnp.sum(h * g, axis=1, keepdims=True) for (h, _), g in zip(blocks, scaled))
    inner_ref[...] = inner
    lessen = scale * scale * scale * (inner / (width * count))
    for s in range(count):
        at = span(offset_ref[s], width)
        branch_ref[:, at] = (
            cot_ref[:, at].astype(F32) + scale * scaled[s] - blocks[s][0] * lessen
        ).astype(BF)
    mixed_ref[...] = wide_dot(branch_ref, weights, dot_cols, 1).astype(BF)


def attend_back_kernel(head, tile, peers, *refs):
    each = peers if peers <= 2 else 1
    grad_ref, q_ref, ql_ref, row_ref, col_ref, att_ref, log_ref, qg_ref, cos_ref, sin_ref = refs[:10]
    all_keys, all_values = refs[10 : 10 + each], refs[10 + each : 10 + 2 * each]
    dql_ref, qpart_ref = refs[-4 - 2 * each : -2 - 2 * each]
    dk_refs, dv_refs = refs[-2 - 2 * each : -2 - each], refs[-2 - each : -2]
    dk_sum, dv_sum = refs[-2:]
    column = columns_of(col_ref, peers)
    rows = q_ref.shape[0]
    kv_heads = all_keys[0].shape[-1] // head
    ratio = q_ref.shape[1] // head // kv_heads
    factor = head ** (-0.5)
    dk_sum[...] = jnp.zeros_like(dk_sum)
    dv_sum[...] = jnp.zeros_like(dv_sum)
    gain_part = jnp.zeros((1, head), F32)
    for t in range(rows // tile):
        part = slice(t * tile, (t + 1) * tile)
        extent = (t + 1) * tile
        grad_mixed = grad_ref[part, :]
        grad_back = jnp.transpose(grad_mixed.astype(F32))
        seq_row, pos_row = row_ref[0:1, part], row_ref[1:2, part]

        def bias_of(p):
            one = visible_bias(*column(p, extent), seq_row, pos_row)
            return jnp.concatenate([one] * ratio, axis=1)

        biases = [bias_of(p) for p in range(peers)] if peers <= 2 else None
        for j in range(kv_heads):
            cut = slice(j * head, (j + 1) * head)
            heads = [j * ratio + i for i in range(ratio)]
            lanes = [slice(h * head, (h + 1) * head) for h in heads]
            queries = jnp.concatenate([q_ref[part, lane] for lane in lanes], axis=0)
            grad_heads = jnp.concatenate([grad_mixed[:, lane] for lane in lanes], axis=0)
            logs = jnp.concatenate([log_ref[h : h + 1, part] for h in heads], axis=1)
            delta = jnp.concatenate(
                [
                    jnp.sum(grad_back[lane, :] * att_ref[lane, part], axis=0, keepdims=True)
                    for lane in lanes
                ],
                axis=1,
            )

            def step(p, accum, bias=None):
                if bias is None:
                    bias = bias_of(p)
                keys = peer_block(all_keys, p, extent, cut)
                values = peer_block(all_values, p, extent, cut)
                probs = jnp.exp(dot_cols(keys, queries) * factor + bias - logs)
                grad_probs = dot_cols(values, grad_heads)
                grad_scores = (probs * (grad_probs - delta)).astype(BF)
                dv_sum[p, :extent, cut] += dot(probs.astype(BF), grad_heads)
                dk_sum[p, :extent, cut] += dot(grad_scores, queries)
                return accum + dot_rows(keys, grad_scores)

            accum = jnp.zeros((head, ratio * tile), F32)
            if peers <= 2:
                for p in range(peers):
                    accum = step(p, accum, biases[p])
            else:
                accum = lax.fori_loop(0, peers, step, accum)
            grad_query = jnp.transpose(accum) * factor
            for i, lane in enumerate(lanes):
                lin, one = unrotate(
                    grad_query[i * tile : (i + 1) * tile, :],
                    ql_ref[part, lane],
                    qg_ref[...],
                    cos_ref[part, :],
                    sin_ref[part, :],
                )
                dql_ref[part, lane] = lin.astype(BF)
                gain_part = gain_part + one
    qpart_ref[...] = gain_part
    for p in range(each):
        at = p if each > 1 or peers == 1 else slice(None)
        dk_refs[p][...] = (dk_sum[at] * factor).astype(BF)
        dv_refs[p][...] = dv_sum[at].astype(BF)


def lin_back_kernel(count, parts_in, head, terms, fused, offset_ref, *refs):
    dql_ref, ql_ref, kl_ref, v_ref, qpart_ref = refs[:5]
    dks, dvs = refs[5 : 5 + terms], refs[5 + terms : 5 + 2 * terms]
    kg_ref, cos_ref, sin_ref = refs[5 + 2 * terms : 8 + 2 * terms]
    weights = refs[8 + 2 * terms : 8 + 2 * terms + 3 * parts_in]
    wq, wk, wv = weights[:parts_in], weights[parts_in : 2 * parts_in], weights[2 * parts_in :]
    turned_ref = refs[8 + 2 * terms + 3 * parts_in] if fused else None
    outs = refs[-count - 2 :]
    parts, (dkl_ref, dvl_ref) = outs[:count], outs[count:]
    shares = refs[-count - 4 : -count - 2]
    rows, width = ql_ref.shape[0], parts[0].shape[1]
    gain_part = jnp.zeros((1, head), F32)
    inners = []
    for i in range(rows // width):
        at = slice(i * width, (i + 1) * width)
        grad_keys = sum(r[at, :].astype(F32) for r in dks)
        dvl_ref[at, :] = sum(r[at, :].astype(F32) for r in dvs).astype(BF)
        for h in range(kl_ref.shape[1] // head):
            cut = slice(h * head, (h + 1) * head)
            lin, one = unrotate(
                grad_keys[:, cut], kl_ref[at, cut], kg_ref[...], cos_ref[at, :], sin_ref[at, :]
            )
            dkl_ref[at, cut] = lin.astype(BF)
            gain_part = gain_part + one
        grad_q, grad_k, grad_v = dql_ref[at, :], dkl_ref[at, :], dvl_ref[at, :]
        inner = (
            jnp.sum(grad_q.astype(F32) * ql_ref[at, :], axis=1, keepdims=True)
            + jnp.sum(grad_k.astype(F32) * kl_ref[at, :], axis=1, keepdims=True)
            + jnp.sum(grad_v.astype(F32) * v_ref[at, :].astype(F32), axis=1, keepdims=True)
        )
        inners.append(jnp.transpose(jnp.broadcast_to(inner, (width, 128)))[0:1, :])
        for s in range(count):
            block = offset_ref[count + s]
            term = (
                dot_cols(grad_q, pick(wq, block, width, 0))
                + dot_cols(grad_k, pick(wk, block, width, 0))
                + dot_cols(grad_v, pick(wv, block, width, 0))
            )
            parts[s][at, :] = term.astype(parts[s].dtype)
    if fused:
        blocks, size, _ = shares[0].shape
        for c in range(blocks):
            at = slice(c * 2 * size, (c + 1) * 2 * size)
            start = 0
            for ref in (dql_ref, dkl_ref, dvl_ref):
                stop = start + ref.shape[1]
                both = dot(turned_ref[at, :], ref[...]).astype(BF)
                for k in range(2):
                    block = 2 * c + k
                    shares[block // blocks][block % blocks, :, start:stop] = both[
                        k * size : (k + 1) * size
                    ]
                start = stop
    inners.append(jnp.concatenate([qpart_ref[...], gain_part], axis=1))
    high = [v.astype(BF).astype(F32) for v in inners]
    low = [v - h for v, h in zip(inners, high)]
    lines = high[:-1] + low[:-1] + [high[-1], low[-1]]
    lines.append(jnp.zeros((16 - len(lines), width), F32))
    below = jnp.concatenate(lines, axis=0)
    for ref in parts:
        ref[rows : rows + 16, :] = below.astype(ref.dtype)


def out(shape, dtype):
    return jax.ShapeDtypeStruct(shape, dtype)


def rows_block(tile, width):
    return pl.BlockSpec((tile, width), lambda i: (i, 0))


def same_block(shape):
    return pl.BlockSpec(shape, lambda i: (0,) * len(shape))


def call(kernel, grid, in_specs, out_specs, out_shape, scratch=(), deps=(), prefetch=0):
    deps = list(deps)
    in_specs = in_specs + [ANY] * len(deps)
    extra = dict(
        in_specs=in_specs, out_specs=out_specs, scratch_shapes=scratch, **(dict(grid=grid) if grid else {})
    )
    if prefetch:
        extra = dict(
            grid_spec=pltpu.PrefetchScalarGridSpec(
                num_scalar_prefetch=prefetch,
                grid=grid,
                in_specs=in_specs,
                out_specs=out_specs,
                scratch_shapes=scratch,
            )
        )
    run = pl.pallas_call(
        kernel,
        out_shape=out_shape,
        compiler_params=pltpu.CompilerParams(vmem_limit_bytes=60 * 2**20),
        cost_estimate=pl.CostEstimate(flops=2**20, bytes_accessed=2**16, transcendentals=0),
        **extra,
    )
    return lambda *args: run(*args, *deps)


def weight_grads(pairs, deps=(), late=()):
    peers, blocks = lax.axis_size("gy"), lax.axis_size("dev")
    rows = pairs[0][1].shape[0]
    turned = [left.shape[1] == rows for left, _ in pairs]
    width = pairs[0][0].size // rows
    size = width // peers // blocks
    total = sum(right.shape[1] for _, right in pairs)
    if peers != 2:
        share = [(dot if t else dot_rows)(a, b) for t, (a, b) in zip(turned, pairs)]
        share = jnp.concatenate(share, axis=1).astype(BF)
        share = lax.psum_scatter(share, "gy", scatter_dimension=0, tiled=True)
        return share.reshape(blocks, size, total), None
    specs, operands = [], []
    for across, (left, right) in zip(turned, pairs):
        if across:
            specs += [
                pl.BlockSpec((size, rows), lambda c: (c, 0)),
                pl.BlockSpec((size, rows), lambda c: (blocks + c, 0)),
            ]
        else:
            specs += [
                pl.BlockSpec((rows, size), lambda c: (0, c)),
                pl.BlockSpec((rows, size), lambda c: (0, blocks + c)),
            ]
        specs.append(pl.BlockSpec(right.shape, lambda c: (0, 0)))
        operands += [left, left, right]
    chunk = pl.BlockSpec((1, size, total), lambda c: (c, 0, 0))
    own, other = call(
        functools.partial(weight_grad_kernel, turned),
        (blocks,),
        specs,
        [chunk, chunk],
        [out((blocks, size, total), BF), out((blocks, size, total), BF)],
        deps=deps,
    )(*operands)
    (other,) = after([other], *late)
    return own, shifted(other, "gy", 1)


def share_chunks(shares, deps=()):
    blocks, size, _ = shares[0][0].shape
    total = sum(own.shape[2] for own, _ in shares)
    if shares[0][1] is None:
        side = jnp.concatenate([own for own, _ in shares], axis=2)
        cut = lambda m: lax.dynamic_index_in_dim(side, dev_partner(m), 0, False)
        return [cut(0).astype(F32)] + [cut(m) for m in range(1, blocks)]
    chunks = jnp.stack([dev_partner(m) for m in range(blocks)]).astype(jnp.int32)
    return call(
        functools.partial(share_sum_kernel, len(shares)),
        None,
        [SMEM] + [VMEM] * (2 * len(shares)),
        [VMEM] * blocks,
        [out((size, total), F32)] + [out((size, total), BF)] * (blocks - 1),
        deps=deps,
    )(chunks, *[own for own, _ in shares], *[got for _, got in shares])


def dev_total(chunks):
    got = [dev_send(part, m) for m, part in enumerate(chunks[1:], 1)]
    total = chunks[0]
    for part in got:
        total = total + part.astype(F32)
    return total, got


def dev_all(total, deps=()):
    (sent,) = after([total.astype(BF)], *deps)
    return [dev_send(sent, m) for m in range(1, lax.axis_size("dev"))]


def widen(whole, pieces, deps=()):
    rows = whole.shape[0]
    shapes = [(w, rows) if turned else (rows, w) for _, w, turned in pieces]
    return call(
        functools.partial(widen_kernel, pieces),
        None,
        [VMEM],
        [VMEM] * len(pieces),
        [out(shape, F32) for shape in shapes],
        deps=deps,
    )(whole)


def assemble(total, others, pieces, deps=()):
    size, blocks = total.shape[0], 1 + len(others)
    owners = jnp.stack([lax.axis_index("dev")] + [dev_giver(m) for m in range(1, blocks)])
    shapes = [(w, size * blocks) if turned else (size * blocks, w) for _, w, turned in pieces]
    widest = max([w for _, w, turned in pieces if turned], default=128)
    return call(
        functools.partial(assemble_kernel, blocks, pieces),
        None,
        [SMEM] + [VMEM] * blocks,
        [VMEM] * len(pieces),
        [out(shape, F32) for shape in shapes],
        [pltpu.VMEM((size * blocks, widest), F32)],
        deps,
    )(owners.astype(jnp.int32), total, *others)


def per_device(
    tokens,
    norm_gain,
    w_query,
    key_projection,
    value_projection,
    query_gain,
    key_gain,
    w_out,
    ffn_gain,
    w_gate,
    w_up,
    w_down,
    cotangent,
    sequence,
    position,
):
    rows, piece = tokens.shape
    count = lax.axis_size("gx")
    peers = lax.axis_size("gy")
    width = piece * count
    head = query_gain.shape[0]
    q_cols, kv_cols, hidden_units = w_query.shape[1], key_projection.shape[1], w_gate.shape[1]
    gx, gy = lax.axis_index("gx"), lax.axis_index("gy")
    tile = min(256, rows)
    small_tile = min(128, rows)
    grid = (rows // tile,)

    def lies_at(block):
        if peers == 2 and count % 2 == 0:
            half = count // 2
            return ((block // half) ^ gy) * (half * piece) + (block % half) * piece
        return block * piece

    offsets = jnp.stack(
        [lies_at((gx - s) % count) for s in range(count)]
        + [lies_at((gx + s) % count) for s in range(count)]
    ).astype(jnp.int32)

    below = jnp.stack([norm_gain, ffn_gain] + [norm_gain] * 14)
    token_pieces = pieces_of(jnp.concatenate([tokens, below], axis=0))
    gain_block = pl.BlockSpec((16, piece), lambda i: (rows // 16, 0))
    query_parts, key_w_parts, value_w_parts = (
        gather_width(w, 0) for w in (w_query, key_projection, value_projection)
    )
    out_w_parts, down_parts = gather_width(w_out, 1), gather_width(w_down, 1)
    gate_parts, up_parts = gather_width(w_gate, 0), gather_width(w_up, 0)
    halves = len(gate_parts)

    all_seq, all_pos = sequence.reshape(peers, rows), position.reshape(peers, rows)
    if peers == 2:
        order = lambda a: jnp.where(gy == 0, a, a[::-1])
        all_seq, all_pos = order(all_seq), order(all_pos)
        own_seq, own_pos = all_seq[0], all_pos[0]
    else:
        own_seq = lax.dynamic_index_in_dim(all_seq, gy, 0, False)
        own_pos = lax.dynamic_index_in_dim(all_pos, gy, 0, False)
    row_info = jnp.concatenate(
        [own_seq[None], own_pos[None], jnp.zeros((6, rows), jnp.int32)], axis=0
    ).astype(F32)
    if peers == 2:
        col_info = jnp.concatenate(
            [all_seq[:1], all_pos[:1], all_seq[1:], all_pos[1:], jnp.zeros((4, rows), jnp.int32)],
            axis=0,
        ).astype(F32)
    else:
        col_info = jnp.stack([all_seq, all_pos], axis=-1).astype(F32)
    lane = jnp.arange(head)
    rates = THETA ** (-((lane % (head // 2)).astype(F32) * 2.0) / head)
    phase = own_pos.astype(F32)[:, None] * rates[None, :]
    cosine = jnp.cos(phase)
    sine = jnp.sin(phase) * jnp.where(lane < head // 2, -1.0, 1.0)[None, :]
    q_scale = query_gain.astype(F32)[None]
    k_scale = key_gain.astype(F32)[None]

    def whole(parts):
        return [same_block(p.shape) for p in parts]

    normed_one, scale_one, query_lin, key_lin, query_bf, key_bf, value_bf = call(
        functools.partial(qkv_kernel, count, halves, head),
        grid,
        [SMEM]
        + [rows_block(tile, piece)] * count
        + [gain_block] * count
        + whole(query_parts + key_w_parts + value_w_parts)
        + [same_block((1, head))] * 2
        + [rows_block(tile, head)] * 2,
        [
            rows_block(tile, width),
            rows_block(tile, 1),
            rows_block(tile, q_cols),
            rows_block(tile, kv_cols),
            rows_block(tile, q_cols),
            rows_block(tile, kv_cols),
            rows_block(tile, kv_cols),
        ],
        [
            out((rows, width), BF),
            out((rows, 1), F32),
            out((rows, q_cols), F32),
            out((rows, kv_cols), F32),
            out((rows, q_cols), BF),
            out((rows, kv_cols), BF),
            out((rows, kv_cols), BF),
        ],
        deps=[row_info, col_info],
    )(
        offsets, *token_pieces, *token_pieces, *query_parts, *key_w_parts, *value_w_parts,
        q_scale, k_scale, cosine, sine,
    )
    if peers == 2:
        keys = [key_bf, shifted(key_bf, "gy", 1)]
        values = [value_bf, shifted(value_bf, "gy", 1)]
    else:
        keys = [lax.all_gather(key_bf, "gy", axis=0)]
        values = [lax.all_gather(value_bf, "gy", axis=0)]
    (late_cotangent,) = after([cotangent], *token_pieces[1:])
    cot_pieces = [cotangent] + pieces_of(late_cotangent)[1:]

    mixed, attended, logs = call(
        functools.partial(attend_kernel, head, small_tile, peers),
        None,
        [VMEM] * (3 + 2 * len(keys)),
        [VMEM] * 3,
        [
            out((rows, q_cols), BF),
            out((q_cols, rows), F32),
            out((max(8, q_cols // head), rows), F32),
        ],
        deps=[cot_pieces[1], cot_pieces[-1]],
    )(query_bf, row_info, col_info, *keys, *values)

    split_out = [out((rows, piece), F32)] + [out((rows, piece), BF)] * (count - 1)

    def split_dot(left, weights, *deps):
        return call(
            functools.partial(split_dot_kernel, count, halves),
            grid,
            [SMEM, rows_block(tile, left.shape[1])] + whole(weights),
            [rows_block(tile, piece)] * count,
            split_out,
            deps=deps,
        )(offsets, left, *weights)

    out_parts = split_dot(mixed, out_w_parts, *cot_pieces[1:])
    inputs = tokens.astype(F32)
    hidden = inputs + piece_sum(out_parts[0], out_parts[1:])

    cot_whole, grad_product, normed_turned = call(
        functools.partial(cot_kernel, count),
        grid,
        [SMEM] + [rows_block(tile, piece)] * count + [rows_block(tile, width)] + whole(down_parts),
        [
            rows_block(tile, width),
            rows_block(tile, hidden_units),
            pl.BlockSpec((width, tile), lambda i: (0, i)),
        ],
        [out((rows, width), BF), out((rows, hidden_units), F32), out((width, rows), BF)],
    )(offsets, *cot_pieces, normed_one, *down_parts)

    hidden_pieces = pieces_of(hidden.astype(BF))
    *grad_parts, normed_two, scale_two, product, gate_bf, up_bf = call(
        functools.partial(ffn_kernel, count, halves),
        grid,
        [SMEM]
        + [rows_block(tile, piece)] * count
        + [gain_block] * count
        + whole(gate_parts + up_parts)
        + [rows_block(tile, hidden_units)],
        [rows_block(tile, piece)] * count
        + [rows_block(tile, width), rows_block(tile, 1)]
        + [rows_block(tile, hidden_units)] * 3,
        split_out
        + [out((rows, width), BF), out((rows, 1), F32)]
        + [out((rows, hidden_units), BF)] * 3,
    )(offsets, *hidden_pieces, *token_pieces, *gate_parts, *up_parts, grad_product)

    grad_got = [shifted(p, "gx", s) for s, p in enumerate(grad_parts[1:], 1)]
    ffn_own, ffn_got = weight_grads(
        [(normed_two, gate_bf), (normed_two, up_bf), (cot_whole, product)], late=grad_got
    )
    grad_normed_two = grad_parts[0]
    for part in grad_got:
        grad_normed_two = grad_normed_two + part.astype(F32)
    (grad_low,) = after([grad_normed_two.astype(BF)], ffn_own)
    grad_pieces = [grad_low] + pieces_of(grad_low)[1:]
    blocks, size, total = ffn_own.shape
    if peers == 2:
        row_tile = rows // blocks
        chunk = pl.BlockSpec((1, size, total), lambda i: (i, 0, 0))
        *result_parts, ffn_share = call(
            functools.partial(result_share_kernel, count, halves),
            (blocks,),
            [SMEM, rows_block(row_tile, hidden_units)] + whole(down_parts) + [chunk, chunk],
            [rows_block(row_tile, piece)] * count + [rows_block(size, total)],
            split_out + [out((blocks * size, total), BF)],
            deps=grad_got,
        )(offsets, product, *down_parts, ffn_own, ffn_got)
    else:
        result_parts = split_dot(product, down_parts)
        ffn_share = ffn_own.reshape(blocks * size, total)
    (ffn_share,) = after([ffn_share], *grad_pieces[1:])
    ffn_chunk = lax.psum_scatter(ffn_share, "dev", scatter_dimension=0, tiled=True)

    branch, grad_mixed, inner_two = call(
        functools.partial(branch_kernel, count, halves),
        grid,
        [SMEM]
        + [rows_block(tile, piece)] * (2 * count)
        + [gain_block] * count
        + [rows_block(tile, 1), rows_block(tile, width)]
        + whole(out_w_parts),
        [rows_block(tile, width), rows_block(tile, q_cols), rows_block(tile, 1)],
        [out((rows, width), BF), out((rows, q_cols), BF), out((rows, 1), F32)],
    )(
        offsets, *hidden_pieces, *grad_pieces, *token_pieces, scale_two, cot_whole, *out_w_parts
    )

    late_parts = after(result_parts[1:], *grad_pieces[1:])
    result_got = [shifted(p, "gx", s) for s, p in enumerate(late_parts, 1)]
    result = hidden + result_parts[0]
    for part in result_got:
        result = result + part.astype(F32)
    out_own, out_got = weight_grads([(branch, mixed)])

    grad_query_lin, query_gain_part, *kv_parts = call(
        functools.partial(attend_back_kernel, head, small_tile, peers),
        None,
        [VMEM] * (10 + 2 * len(keys)),
        [VMEM] * (2 + 2 * len(keys)),
        [out((rows, q_cols), BF), out((1, head), F32)]
        + [out(k.shape, BF) for k in keys + values],
        [pltpu.VMEM((peers, rows, kv_cols), F32), pltpu.VMEM((peers, rows, kv_cols), F32)],
        deps=[out_own, result_got[0], result_got[-1]],
    )(
        grad_mixed, query_bf, query_lin, row_info, col_info, attended, logs,
        q_scale, cosine, sine, *keys, *values,
    )
    if peers == 2:
        key_terms = [kv_parts[0], shifted(kv_parts[1], "gy", 1)]
        value_terms = [kv_parts[2], shifted(kv_parts[3], "gy", 1)]
    else:
        share = lambda a: lax.psum_scatter(a, "gy", scatter_dimension=0, tiled=True)[0]
        key_terms, value_terms = [share(kv_parts[0])], [share(kv_parts[1])]

    fused = peers == 2
    shares = [out(out_own.shape[:2] + (q_cols + 2 * kv_cols,), BF)] * 2 if fused else []
    *last_outs, grad_key_lin, grad_value_lin = call(
        functools.partial(lin_back_kernel, count, halves, head, len(key_terms), fused),
        None,
        [SMEM] + [VMEM] * (8 + 2 * len(key_terms) + 3 * halves + fused),
        [VMEM] * (count + 2 + len(shares)),
        shares
        + [out((rows + 16, piece), p.dtype) for p in split_out]
        + [out((rows, kv_cols), BF)] * 2,
        deps=result_got[1:-1],
    )(
        offsets, grad_query_lin, query_lin, key_lin, value_bf, query_gain_part,
        *key_terms, *value_terms, k_scale, cosine, sine,
        *query_parts, *key_w_parts, *value_w_parts, *([normed_turned] if fused else []),
    )
    last_parts = last_outs[len(shares) :]
    last_got = [shifted(p, "gx", s) for s, p in enumerate(last_parts[1:], 1)]
    if fused:
        last_share = last_outs[0], shifted(last_outs[1], "gy", 1)
    else:
        last_share = weight_grads(
            [(normed_turned, g) for g in (grad_query_lin, grad_key_lin, grad_value_lin)]
        )
    last_chunks = share_chunks([last_share, (out_own, out_got)])
    (ffn_low,) = after([ffn_chunk], last_chunks[1])
    ffn_sum = lax.all_gather(ffn_low, "dev", axis=0, tiled=True)
    last_total, dev_got = dev_total(last_chunks)
    last_others = dev_all(last_total)
    gate_grad, up_grad, down_grad = widen(
        ffn_sum,
        (
            (0, hidden_units, False),
            (hidden_units, hidden_units, False),
            (2 * hidden_units, hidden_units, True),
        ),
        [last_total],
    )
    cuts = (0, q_cols, q_cols + kv_cols, q_cols + 2 * kv_cols)
    query_grad, key_grad, value_grad, out_grad = assemble(
        last_total,
        last_others,
        (
            (cuts[0], q_cols, False),
            (cuts[1], kv_cols, False),
            (cuts[2], kv_cols, False),
            (cuts[3], q_cols, True),
        ),
        [down_grad],
    )

    grad_inputs, gain_part = call(
        functools.partial(final_kernel, count),
        None,
        [VMEM] * (count + 8),
        [VMEM] * 2,
        [out((rows, piece), F32), out((8, piece), F32)],
        deps=dev_got[:1],
    )(
        last_parts[0], *last_got, tokens, cotangent, hidden, grad_normed_two,
        scale_one, scale_two, inner_two, below,
    )
    if peers == 2:
        last = small_sum(small_sum(gain_part, "gy"), "dev")
    else:
        last = lax.psum(gain_part, ("dev", "gy"))
    return (
        result.astype(BF),
        grad_inputs,
        last[0],
        query_grad,
        key_grad,
        value_grad,
        last[2, :head],
        last[2, head : 2 * head],
        out_grad,
        last[1],
        gate_grad,
        up_grad,
        down_grad,
    )


def solution(mesh):
    wide = P(("dev", "gy"), "gx")
    weight, back = P("gy", "gx"), P("gx", "gy")
    return jax.shard_map(
        per_device,
        mesh=mesh,
        in_specs=(
            wide, P("gx"), weight, weight, weight, P(), P(), back, P("gx"), weight, weight, back,
            wide, P("dev"), P("dev"),
        ),
        out_specs=(
            wide, wide, P("gx"), weight, weight, weight, P(), P(), back, P("gx"), weight, weight,
            back,
        ),
        check_vma=False,
    )
```

```python
import functools

import jax
import jax.numpy as jnp
from jax import lax
from jax.experimental import pallas as pl
from jax.experimental.pallas import tpu as pltpu
from jax.sharding import PartitionSpec as P

EPS = 1e-06
THETA = 1000000.0
NEGATIVE = -1e30
BF = jnp.bfloat16
F32 = jnp.float32
VMEM = pl.BlockSpec(memory_space=pltpu.VMEM)
SMEM = pl.BlockSpec(memory_space=pltpu.SMEM)
ANY = pl.BlockSpec(memory_space=pl.ANY)


def dot(left, right):
    return lax.dot_general(left, right, (((1,), (0,)), ((), ())), preferred_element_type=F32)


def dot_cols(left, right):
    return lax.dot_general(left, right, (((1,), (1,)), ((), ())), preferred_element_type=F32)


def dot_rows(left, right):
    return lax.dot_general(left, right, (((0,), (0,)), ((), ())), preferred_element_type=F32)


def span(offset, size):
    return pl.ds(pl.multiple_of(offset, size), size)


def turn(vectors):
    return pltpu.roll(vectors, vectors.shape[-1] // 2, 1)


def shifted(block, axis, shift):
    size = lax.axis_size(axis)
    return lax.ppermute(block, axis, [(i, (i + shift) % size) for i in range(size)])


def pieces_of(block):
    return [block] + [shifted(block, "gx", s) for s in range(1, lax.axis_size("gx"))]


def piece_sum(own, others):
    total = own
    for s, part in enumerate(others, 1):
        total = total + shifted(part, "gx", s).astype(F32)
    return total


def gather_width(block, axis):
    if lax.axis_size("gy") == 2:
        return [block, shifted(block, "gy", 1)]
    return [lax.all_gather(block, "gy", axis=axis, tiled=True)]


def dev_partner(m):
    count, here = lax.axis_size("dev"), lax.axis_index("dev")
    return here ^ m if count & (count - 1) == 0 else (here + m) % count


def dev_giver(m):
    count, here = lax.axis_size("dev"), lax.axis_index("dev")
    return here ^ m if count & (count - 1) == 0 else (here - m) % count


def dev_send(block, m):
    count = lax.axis_size("dev")
    even = count & (count - 1) == 0
    return lax.ppermute(
        block, "dev", [(i, i ^ m if even else (i + m) % count) for i in range(count)]
    )


def nothing(*refs):
    pass


def after(arrays, *deps):
    if not deps or not arrays:
        return arrays
    return pl.pallas_call(
        nothing,
        in_specs=[ANY] * (len(arrays) + len(deps)),
        out_specs=[ANY] * len(arrays),
        out_shape=[jax.ShapeDtypeStruct(a.shape, a.dtype) for a in arrays],
        input_output_aliases={i: i for i in range(len(arrays))},
    )(*arrays, *deps)


def small_sum(block, axis):
    total = block
    for s in range(1, lax.axis_size(axis)):
        total = total + shifted(block, axis, s)
    return total


def pick(refs, offset, size, axis):
    half = refs[0].shape[axis]

    def cut(ref):
        at = span(offset % half, size)
        return ref[at, :] if axis == 0 else ref[:, at]

    if len(refs) == 1:
        return cut(refs[0])
    return jnp.where(offset < half, cut(refs[0]), cut(refs[1]))


def wide_dot(left_ref, refs, product, axis):
    step = left_ref.shape[1] // len(refs)
    return sum(
        product(left_ref[:, i * step : (i + 1) * step], ref[...]) for i, ref in enumerate(refs)
    )


def normalise(pieces, gains, row, offset_ref, normed_ref, scale_ref):
    count, width = len(pieces), pieces[0].shape[1]
    blocks = [p[...].astype(F32) for p in pieces]
    square = sum(jnp.sum(b * b, axis=1, keepdims=True) for b in blocks)
    scale = lax.rsqrt(square / (width * count) + EPS)
    scale_ref[...] = scale
    for s in range(count):
        gain = gains[s][row : row + 1, :].astype(F32)
        normed_ref[:, span(offset_ref[s], width)] = (blocks[s] * scale * gain).astype(BF)


def prepare_kernel(seq_ref, pos_ref, rate_ref, row_ref, col_ref, cos_ref, sin_ref):
    rows, head = cos_ref.shape
    here = lax.axis_index("gy")
    lines = []
    for peer in (here, 1 - here):
        at = span(peer * rows, rows)
        lines += [seq_ref[:, at].astype(F32), pos_ref[:, at].astype(F32)]
    row_ref[...] = jnp.concatenate(lines[:2] + [jnp.zeros((6, rows), F32)], axis=0)
    col_ref[...] = jnp.concatenate(lines + [jnp.zeros((4, rows), F32)], axis=0)
    place = jnp.transpose(col_ref[...])[:, 1:2]
    phase = place * rate_ref[...]
    lane = lax.broadcasted_iota(jnp.int32, (rows, head), 1)
    cos_ref[...] = jnp.cos(phase)
    sine = jnp.sin(phase)
    sin_ref[...] = jnp.where(lane < head // 2, -sine, sine)


def cot_kernel(count, offset_ref, *refs):
    pieces, normed_ref, downs = refs[:count], refs[count], refs[count + 1 : -5]
    whole_ref, grad_ref, turned_ref, cot_turned_ref, cot_sent_ref = refs[-5:]
    turned_ref[...] = jnp.transpose(normed_ref[...])
    width = pieces[0].shape[1]
    for s in range(count):
        whole_ref[:, span(offset_ref[s], width)] = pieces[s][...]
    half = whole_ref.shape[1] // 2
    cot_turned_ref[...] = jnp.transpose(whole_ref[:, :half])
    cot_sent_ref[...] = jnp.transpose(whole_ref[:, half:])
    grad_ref[...] = wide_dot(whole_ref, downs, dot_cols, 1)


def qkv_kernel(count, parts, head, offset_ref, *refs):
    pieces, gains, refs = refs[:count], refs[count : 2 * count], refs[2 * count :]
    wq, wk, wv = refs[:parts], refs[parts : 2 * parts], refs[2 * parts : 3 * parts]
    qg_ref, kg_ref, cos_ref, sin_ref = refs[3 * parts : 3 * parts + 4]
    normed_ref, scale_ref, ql_ref, kl_ref, q_ref, k_ref, v_ref = refs[-7:]
    normalise(pieces, gains, 0, offset_ref, normed_ref, scale_ref)
    ql_ref[...] = wide_dot(normed_ref, wq, dot, 0)
    kl_ref[...] = wide_dot(normed_ref, wk, dot, 0)
    v_ref[...] = wide_dot(normed_ref, wv, dot, 0).astype(BF)
    cosine, sine = cos_ref[...], sin_ref[...]
    for lin_ref, gain, out_ref in ((ql_ref, qg_ref, q_ref), (kl_ref, kg_ref, k_ref)):
        for h in range(lin_ref.shape[1] // head):
            cut = slice(h * head, (h + 1) * head)
            u = lin_ref[:, cut]
            u = u * lax.rsqrt(jnp.mean(u * u, axis=1, keepdims=True) + EPS) * gain[...]
            out_ref[:, cut] = (u * cosine + turn(u) * sine).astype(BF)


def visible_bias(seq_col, pos_col, seq_row, pos_row):
    seen = (seq_col == seq_row) & (pos_col <= pos_row)
    return jnp.where(seen, 0.0, NEGATIVE)


def peer_block(refs, p, extent, cut):
    return refs[p][:extent, cut] if len(refs) > 1 else refs[0][p, :extent, cut]


def columns_of(col_ref, peers):
    if peers > 2:
        return lambda p, extent: (col_ref[p, :extent, 0:1], col_ref[p, :extent, 1:2])
    turned = jnp.transpose(col_ref[...])
    return lambda p, extent: (
        turned[:extent, 2 * p : 2 * p + 1],
        turned[:extent, 2 * p + 1 : 2 * p + 2],
    )


def attend_kernel(head, tile, peers, q_ref, row_ref, col_ref, *refs):
    each = peers if peers <= 2 else 1
    keys, values = refs[:each], refs[each : 2 * each]
    mixed_ref, att_ref, log_ref = refs[-3:]
    column = columns_of(col_ref, peers)
    rows = q_ref.shape[0]
    kv_heads = keys[0].shape[-1] // head
    ratio = q_ref.shape[1] // head // kv_heads
    factor = head ** (-0.5)
    for t in range(rows // tile):
        part = slice(t * tile, (t + 1) * tile)
        extent = (t + 1) * tile
        seq_row, pos_row = row_ref[0:1, part], row_ref[1:2, part]

        def bias_of(p):
            one = visible_bias(*column(p, extent), seq_row, pos_row)
            return jnp.concatenate([one] * ratio, axis=1)

        biases = [bias_of(p) for p in range(peers)] if peers <= 2 else None
        for j in range(kv_heads):
            cut = slice(j * head, (j + 1) * head)
            queries = jnp.concatenate(
                [
                    q_ref[part, (j * ratio + i) * head : (j * ratio + i + 1) * head]
                    for i in range(ratio)
                ],
                axis=0,
            )

            def step(p, carry, bias=None):
                high, total, accum = carry
                if bias is None:
                    bias = bias_of(p)
                scores = dot_cols(peer_block(keys, p, extent, cut), queries) * factor + bias
                newest = jnp.maximum(high, jnp.max(scores, axis=0, keepdims=True))
                weights = jnp.exp(scores - newest)
                shrink = jnp.exp(high - newest)
                total = total * shrink + jnp.sum(weights, axis=0, keepdims=True)
                accum = accum * shrink + dot_rows(
                    peer_block(values, p, extent, cut), weights.astype(BF)
                )
                return newest, total, accum

            carry = (
                jnp.full((1, ratio * tile), NEGATIVE, F32),
                jnp.zeros((1, ratio * tile), F32),
                jnp.zeros((head, ratio * tile), F32),
            )
            if peers <= 2:
                for p in range(peers):
                    carry = step(p, carry, biases[p])
            else:
                carry = lax.fori_loop(0, peers, step, carry)
            high, total, accum = carry
            attended = accum / total
            logs = high + jnp.log(total)
            back = jnp.transpose(attended)
            for i in range(ratio):
                h = j * ratio + i
                lane = slice(i * tile, (i + 1) * tile)
                att_ref[h * head : (h + 1) * head, part] = attended[:, lane]
                log_ref[h : h + 1, part] = logs[:, lane]
                mixed_ref[part, h * head : (h + 1) * head] = back[lane, :].astype(BF)


def ffn_kernel(count, parts_in, offset_ref, *refs):
    pieces, gains, refs = refs[:count], refs[count : 2 * count], refs[2 * count :]
    wg, wu, grad_ref = refs[:parts_in], refs[parts_in : 2 * parts_in], refs[2 * parts_in]
    outs = refs[-count - 5 :]
    parts, (normed_ref, scale_ref, product_ref, delta_ref, sent_ref) = outs[:count], outs[count:]
    width, units = pieces[0].shape[1], product_ref.shape[1]
    gate_ref, up_ref = delta_ref.at[:, :units], delta_ref.at[:, units : 2 * units]
    normalise(pieces, gains, 1, offset_ref, normed_ref, scale_ref)
    sent_ref[...] = normed_ref[:, normed_ref.shape[1] // 2 :]
    gate = wide_dot(normed_ref, wg, dot, 0)
    up = wide_dot(normed_ref, wu, dot, 0)
    sig = 1.0 / (1.0 + jnp.exp(-gate))
    silu = gate * sig
    product_ref[...] = (silu * up).astype(BF)
    delta_ref[:, 2 * units :] = product_ref[...]
    grad = grad_ref[...]
    gate_ref[...] = (grad * up * (sig + silu * (1.0 - sig))).astype(BF)
    up_ref[...] = (grad * silu).astype(BF)
    for s in range(count):
        at = offset_ref[count + s]
        parts[s][...] = (
            dot_cols(gate_ref[...], pick(wg, at, width, 0))
            + dot_cols(up_ref[...], pick(wu, at, width, 0))
        ).astype(parts[s].dtype)


def split_dot_kernel(count, parts_in, offset_ref, left_ref, *refs):
    weights, parts = refs[:parts_in], refs[-count:]
    width = parts[0].shape[1]
    for s in range(count):
        weight = pick(weights, offset_ref[count + s], width, 1)
        parts[s][...] = dot(left_ref[...], weight).astype(parts[s].dtype)


def ffn_share_kernel(own_ref, got_ref, cot_ref, cot_got_ref, delta_ref, delta_got_ref, share_ref):
    units = share_ref.shape[1] // 3
    left = jnp.transpose(own_ref[...]), jnp.transpose(got_ref[...])
    back = cot_ref[...], cot_got_ref[...]
    for i, pair in enumerate((left, left, back)):
        at = slice(i * units, (i + 1) * units)
        value = dot(pair[0], delta_ref[:, at]) + dot(pair[1], delta_got_ref[:, at])
        share_ref[:, at] = value.astype(BF)


def weight_grad_kernel(groups, *refs):
    own_ref, other_ref = refs[-2:]
    size = own_ref.shape[1]
    start = 0
    for across, rights in groups:
        own, other, refs = refs[0], refs[1], refs[2:]
        left = jnp.concatenate([own[...], other[...]], axis=0 if across else 1)
        if not across:
            left = jnp.transpose(left)
        for right in refs[:rights]:
            width = right.shape[1]
            both = dot(left, right[...]).astype(BF)
            own_ref[0, :, start : start + width] = both[:size]
            other_ref[0, :, start : start + width] = both[size:]
            start += width
        refs = refs[rights:]


def final_kernel(count, *refs):
    parts = refs[:count]
    (tok_ref, cot_ref, hid_ref, two_ref, one_scale, two_scale, two_inner) = refs[count : count + 7]
    grad_ref, part_ref = refs[-2:]
    rows, width = hid_ref.shape
    size = width * count
    gains = tok_ref[rows : rows + 16, :].astype(F32)
    gain_one, gain_two = gains[0:1, :], gains[1:2, :]
    sums = [jnp.zeros((1, width), F32)] * 2
    small = sum(p[rows : rows + 16, :].astype(F32) for p in parts)
    count_rows = rows // width
    for i in range(count_rows):
        at = slice(i * width, (i + 1) * width)
        one = sum(p[at, :].astype(F32) for p in parts)
        inputs, hidden, two = tok_ref[at, :].astype(F32), hid_ref[at, :], two_ref[at, :]
        scale, later = one_scale[at, :], two_scale[at, :]
        inner = small[i : i + 1, :] + small[count_rows + i : count_rows + i + 1, :]
        inner = jnp.transpose(jnp.broadcast_to(inner, (128, width)))[:, 0:1]
        grad_ref[at, :] = (
            cot_ref[at, :].astype(F32)
            + later * (two * gain_two)
            - hidden * (later * later * later * (two_inner[at, :] / size))
            + scale * (one * gain_one)
            - inputs * (scale * scale * (inner / size))
        )
        sums[0] = sums[0] + jnp.sum(one * inputs * scale, axis=0, keepdims=True)
        sums[1] = sums[1] + jnp.sum(two * hidden * later, axis=0, keepdims=True)
    last = 2 * count_rows
    part_ref[...] = jnp.concatenate(
        sums
        + [small[last : last + 1, :] + small[last + 1 : last + 2, :], jnp.zeros((5, width), F32)],
        axis=0,
    )


def share_sum_kernel(shares, chunk_ref, *refs):
    owns, gots = refs[:shares], refs[shares : 2 * shares]
    blocks = owns[0].shape[0]
    for m, ref in enumerate(refs[-blocks:]):
        c = chunk_ref[m]
        start = 0
        for own, got in zip(owns, gots):
            stop = start + own.shape[2]
            ref[:, start:stop] = (own[c].astype(F32) + got[c].astype(F32)).astype(ref.dtype)
            start = stop


def halving_kernel(shares, chunk_ref, *refs):
    owns, gots = refs[:shares], refs[shares : 2 * shares]
    outs = refs[-4:]
    half = outs[0].shape[2]
    start = 0
    for own, got in zip(owns, gots):
        stop = start + own.shape[2]
        for side, (keep, send) in enumerate((outs[:2], outs[2:])):
            low, high = max(start, side * half), min(stop, (side + 1) * half)
            if low >= high:
                continue
            cut, at = slice(low - start, high - start), slice(low - side * half, high - side * half)
            for ref, pair in ((keep, (0, 2 - side)), (send, (1 + side, 3))):
                for k, which in enumerate(pair):
                    c = chunk_ref[which]
                    ref[k, :, at] = (
                        own[c, :, cut].astype(F32) + got[c, :, cut].astype(F32)
                    ).astype(ref.dtype)
        start = stop


def halving_add_kernel(keep_a, got_a, keep_b, got_b, mine_a, send_a, mine_b, send_b):
    for keep, got, mine, send in (
        (keep_a, got_a, mine_a, send_a),
        (keep_b, got_b, mine_b, send_b),
    ):
        mine[...] = keep[0] + got[0].astype(F32)
        send[...] = (keep[1] + got[1].astype(F32)).astype(BF)


def halving_total_kernel(mine_a, got_a, mine_b, got_b, *refs):
    total_ref, low_ref = refs[-2:]
    half = mine_a.shape[1]
    for start, mine, got in ((0, mine_a, got_a), (half, mine_b, got_b)):
        value = mine[...] + got[...].astype(F32)
        total_ref[:, start : start + half] = value
        low_ref[:, start : start + half] = value.astype(BF)


def result_share_kernel(count, parts_in, offset_ref, left_ref, *refs):
    weights, (own_ref, got_ref) = refs[:parts_in], refs[parts_in : parts_in + 2]
    split_dot_kernel(count, parts_in, offset_ref, left_ref, *weights, *refs[-count - 1 : -1])
    refs[-1][...] = (own_ref[0].astype(F32) + got_ref[0].astype(F32)).astype(BF)


def widen_kernel(pieces, whole_ref, *refs):
    for (start, width, turned), ref in zip(pieces, refs[-len(pieces) :]):
        value = whole_ref[:, start : start + width].astype(F32)
        ref[...] = jnp.transpose(value) if turned else value


def assemble_kernel(count, pieces, owner_ref, *refs):
    parts, outs = refs[:count], refs[-len(pieces) - 1 : -1]
    held = refs[-1]
    size = parts[0].shape[0]
    for (start, width, turned), ref in zip(pieces, outs):
        for m, part in enumerate(parts):
            at = pl.ds(pl.multiple_of(owner_ref[m] * size, size), size)
            value = part[:, start : start + width].astype(F32)
            if turned:
                held[at, :width] = value
            else:
                ref[at, :] = value
        if turned:
            ref[...] = jnp.transpose(held[:, :width])


def unrotate(grad, lin, gain, cosine, sine):
    size = lin.shape[1]
    inner = grad * cosine + turn(grad * sine)
    inverse = lax.rsqrt(jnp.mean(lin * lin, axis=1, keepdims=True) + EPS)
    unit = lin * inverse
    part = jnp.sum(inner * unit, axis=0, keepdims=True)
    inner = inner * gain
    mean = jnp.sum(inner * unit, axis=1, keepdims=True) / size
    return inverse * (inner - unit * mean), part


def branch_kernel(count, parts_in, offset_ref, *refs):
    hidden, grads, gains = refs[:count], refs[count : 2 * count], refs[2 * count : 3 * count]
    scale_ref, cot_ref = refs[3 * count : 3 * count + 2]
    weights = refs[3 * count + 2 : 3 * count + 2 + parts_in]
    branch_ref, mixed_ref, inner_ref = refs[-3:]
    width = hidden[0].shape[1]
    scale = scale_ref[...]
    blocks = [(h[...].astype(F32), g[...].astype(F32)) for h, g in zip(hidden, grads)]
    scaled = [g * gain[1:2, :].astype(F32) for gain, (_, g) in zip(gains, blocks)]
    inner = sum(jnp.sum(h * g, axis=1, keepdims=True) for (h, _), g in zip(blocks, scaled))
    inner_ref[...] = inner
    lessen = scale * scale * scale * (inner / (width * count))
    for s in range(count):
        at = span(offset_ref[s], width)
        branch_ref[:, at] = (
            cot_ref[:, at].astype(F32) + scale * scaled[s] - blocks[s][0] * lessen
        ).astype(BF)
    mixed_ref[...] = wide_dot(branch_ref, weights, dot_cols, 1).astype(BF)


def attend_back_kernel(head, tile, peers, *refs):
    each = peers if peers <= 2 else 1
    grad_ref, q_ref, ql_ref, row_ref, col_ref, att_ref, log_ref, qg_ref, cos_ref, sin_ref = refs[:10]
    all_keys, all_values = refs[10 : 10 + each], refs[10 + each : 10 + 2 * each]
    dql_ref, qpart_ref = refs[-4 - 2 * each : -2 - 2 * each]
    dk_refs, dv_refs = refs[-2 - 2 * each : -2 - each], refs[-2 - each : -2]
    dk_sum, dv_sum = refs[-2:]
    column = columns_of(col_ref, peers)
    rows = q_ref.shape[0]
    kv_heads = all_keys[0].shape[-1] // head
    ratio = q_ref.shape[1] // head // kv_heads
    factor = head ** (-0.5)
    dk_sum[...] = jnp.zeros_like(dk_sum)
    dv_sum[...] = jnp.zeros_like(dv_sum)
    gain_part = jnp.zeros((1, head), F32)
    for t in range(rows // tile):
        part = slice(t * tile, (t + 1) * tile)
        extent = (t + 1) * tile
        grad_mixed = grad_ref[part, :]
        grad_back = jnp.transpose(grad_mixed.astype(F32))
        seq_row, pos_row = row_ref[0:1, part], row_ref[1:2, part]

        def bias_of(p):
            one = visible_bias(*column(p, extent), seq_row, pos_row)
            return jnp.concatenate([one] * ratio, axis=1)

        biases = [bias_of(p) for p in range(peers)] if peers <= 2 else None
        for j in range(kv_heads):
            cut = slice(j * head, (j + 1) * head)
            heads = [j * ratio + i for i in range(ratio)]
            lanes = [slice(h * head, (h + 1) * head) for h in heads]
            queries = jnp.concatenate([q_ref[part, lane] for lane in lanes], axis=0)
            grad_heads = jnp.concatenate([grad_mixed[:, lane] for lane in lanes], axis=0)
            logs = jnp.concatenate([log_ref[h : h + 1, part] for h in heads], axis=1)
            delta = jnp.concatenate(
                [
                    jnp.sum(grad_back[lane, :] * att_ref[lane, part], axis=0, keepdims=True)
                    for lane in lanes
                ],
                axis=1,
            )

            def step(p, accum, bias=None):
                if bias is None:
                    bias = bias_of(p)
                keys = peer_block(all_keys, p, extent, cut)
                values = peer_block(all_values, p, extent, cut)
                probs = jnp.exp(dot_cols(keys, queries) * factor + bias - logs)
                grad_probs = dot_cols(values, grad_heads)
                grad_scores = (probs * (grad_probs - delta)).astype(BF)
                dv_sum[p, :extent, cut] += dot(probs.astype(BF), grad_heads)
                dk_sum[p, :extent, cut] += dot(grad_scores, queries)
                return accum + dot_rows(keys, grad_scores)

            accum = jnp.zeros((head, ratio * tile), F32)
            if peers <= 2:
                for p in range(peers):
                    accum = step(p, accum, biases[p])
            else:
                accum = lax.fori_loop(0, peers, step, accum)
            grad_query = jnp.transpose(accum) * factor
            for i, lane in enumerate(lanes):
                lin, one = unrotate(
                    grad_query[i * tile : (i + 1) * tile, :],
                    ql_ref[part, lane],
                    qg_ref[...],
                    cos_ref[part, :],
                    sin_ref[part, :],
                )
                dql_ref[part, lane] = lin.astype(BF)
                gain_part = gain_part + one
    qpart_ref[...] = gain_part
    for p in range(each):
        at = p if each > 1 or peers == 1 else slice(None)
        dk_refs[p][...] = (dk_sum[at] * factor).astype(BF)
        dv_refs[p][...] = dv_sum[at].astype(BF)


def lin_back_kernel(count, parts_in, head, terms, fused, offset_ref, *refs):
    dql_ref, ql_ref, kl_ref, v_ref, qpart_ref = refs[:5]
    dks, dvs = refs[5 : 5 + terms], refs[5 + terms : 5 + 2 * terms]
    kg_ref, cos_ref, sin_ref = refs[5 + 2 * terms : 8 + 2 * terms]
    weights = refs[8 + 2 * terms : 8 + 2 * terms + 3 * parts_in]
    wq, wk, wv = weights[:parts_in], weights[parts_in : 2 * parts_in], weights[2 * parts_in :]
    turned_ref = refs[8 + 2 * terms + 3 * parts_in] if fused else None
    outs = refs[-count - 2 :]
    parts, (dkl_ref, dvl_ref) = outs[:count], outs[count:]
    shares = refs[-count - 4 : -count - 2]
    rows, width = ql_ref.shape[0], parts[0].shape[1]
    gain_part = jnp.zeros((1, head), F32)
    inners = []
    for i in range(rows // width):
        at = slice(i * width, (i + 1) * width)
        grad_keys = sum(r[at, :].astype(F32) for r in dks)
        dvl_ref[at, :] = sum(r[at, :].astype(F32) for r in dvs).astype(BF)
        for h in range(kl_ref.shape[1] // head):
            cut = slice(h * head, (h + 1) * head)
            lin, one = unrotate(
                grad_keys[:, cut], kl_ref[at, cut], kg_ref[...], cos_ref[at, :], sin_ref[at, :]
            )
            dkl_ref[at, cut] = lin.astype(BF)
            gain_part = gain_part + one
        grad_q, grad_k, grad_v = dql_ref[at, :], dkl_ref[at, :], dvl_ref[at, :]
        inner = (
            jnp.sum(grad_q.astype(F32) * ql_ref[at, :], axis=1, keepdims=True)
            + jnp.sum(grad_k.astype(F32) * kl_ref[at, :], axis=1, keepdims=True)
            + jnp.sum(grad_v.astype(F32) * v_ref[at, :].astype(F32), axis=1, keepdims=True)
        )
        inners.append(jnp.transpose(jnp.broadcast_to(inner, (width, 128)))[0:1, :])
        for s in range(count):
            block = offset_ref[count + s]
            term = (
                dot_cols(grad_q, pick(wq, block, width, 0))
                + dot_cols(grad_k, pick(wk, block, width, 0))
                + dot_cols(grad_v, pick(wv, block, width, 0))
            )
            parts[s][at, :] = term.astype(parts[s].dtype)
    if fused:
        blocks, size, _ = shares[0].shape
        for c in range(blocks):
            at = slice(c * 2 * size, (c + 1) * 2 * size)
            start = 0
            for ref in (dql_ref, dkl_ref, dvl_ref):
                stop = start + ref.shape[1]
                both = dot(turned_ref[at, :], ref[...]).astype(BF)
                for k in range(2):
                    block = 2 * c + k
                    shares[block // blocks][block % blocks, :, start:stop] = both[
                        k * size : (k + 1) * size
                    ]
                start = stop
    inners.append(jnp.concatenate([qpart_ref[...], gain_part], axis=1))
    high = [v.astype(BF).astype(F32) for v in inners]
    low = [v - h for v, h in zip(inners, high)]
    lines = high[:-1] + low[:-1] + [high[-1], low[-1]]
    lines.append(jnp.zeros((16 - len(lines), width), F32))
    below = jnp.concatenate(lines, axis=0)
    for ref in parts:
        ref[rows : rows + 16, :] = below.astype(ref.dtype)


def out(shape, dtype):
    return jax.ShapeDtypeStruct(shape, dtype)


def rows_block(tile, width):
    return pl.BlockSpec((tile, width), lambda i: (i, 0))


def same_block(shape):
    return pl.BlockSpec(shape, lambda i: (0,) * len(shape))


def call(kernel, grid, in_specs, out_specs, out_shape, scratch=(), deps=(), aliases=None):
    deps = list(deps)
    in_specs = in_specs + [ANY] * len(deps)
    extra = dict(
        in_specs=in_specs, out_specs=out_specs, scratch_shapes=scratch, **(dict(grid=grid) if grid else {})
    )
    run = pl.pallas_call(
        kernel,
        out_shape=out_shape,
        input_output_aliases=aliases or {},
        compiler_params=pltpu.CompilerParams(vmem_limit_bytes=60 * 2**20),
        cost_estimate=pl.CostEstimate(flops=2**20, bytes_accessed=2**16, transcendentals=0),
        **extra,
    )
    return lambda *args: run(*args, *deps)


def weight_grads(groups):
    peers, blocks = lax.axis_size("gy"), lax.axis_size("dev")
    rows = groups[0][1][0].shape[0]
    turned = [left.shape[1] == rows for left, _ in groups]
    width = groups[0][0].size // rows
    size = width // peers // blocks
    total = sum(right.shape[1] for _, rights in groups for right in rights)
    if peers != 2:
        share = [
            (dot if t else dot_rows)(left, right)
            for t, (left, rights) in zip(turned, groups)
            for right in rights
        ]
        share = jnp.concatenate(share, axis=1).astype(BF)
        share = lax.psum_scatter(share, "gy", scatter_dimension=0, tiled=True)
        return share.reshape(blocks, size, total), None
    specs, operands = [], []
    for across, (left, rights) in zip(turned, groups):
        if across:
            specs += [
                pl.BlockSpec((size, rows), lambda c: (c, 0)),
                pl.BlockSpec((size, rows), lambda c: (blocks + c, 0)),
            ]
        else:
            specs += [
                pl.BlockSpec((rows, size), lambda c: (0, c)),
                pl.BlockSpec((rows, size), lambda c: (0, blocks + c)),
            ]
        specs += [pl.BlockSpec(right.shape, lambda c: (0, 0)) for right in rights]
        operands += [left, left, *rights]
    chunk = pl.BlockSpec((1, size, total), lambda c: (c, 0, 0))
    own, other = call(
        functools.partial(
            weight_grad_kernel, [(t, len(rights)) for t, (_, rights) in zip(turned, groups)]
        ),
        (blocks,),
        specs,
        [chunk, chunk],
        [out((blocks, size, total), BF), out((blocks, size, total), BF)],
    )(*operands)
    return own, shifted(other, "gy", 1)


def share_chunks(shares, deps=()):
    blocks, size, _ = shares[0][0].shape
    total = sum(own.shape[2] for own, _ in shares)
    if shares[0][1] is None:
        side = jnp.concatenate([own for own, _ in shares], axis=2)
        cut = lambda m: lax.dynamic_index_in_dim(side, dev_partner(m), 0, False)
        return [cut(0).astype(F32)] + [cut(m) for m in range(1, blocks)]
    chunks = jnp.stack([dev_partner(m) for m in range(blocks)]).astype(jnp.int32)
    return call(
        functools.partial(share_sum_kernel, len(shares)),
        None,
        [SMEM] + [VMEM] * (2 * len(shares)),
        [VMEM] * blocks,
        [out((size, total), F32)] + [out((size, total), BF)] * (blocks - 1),
        deps=deps,
    )(chunks, *[own for own, _ in shares], *[got for _, got in shares])


def dev_total(chunks):
    got = [dev_send(part, m) for m, part in enumerate(chunks[1:], 1)]
    total = chunks[0]
    for part in got:
        total = total + part.astype(F32)
    return total, got


def halving_total(shares, before, deps):
    blocks, size, _ = shares[0][0].shape
    half = sum(own.shape[2] for own, _ in shares) // 2
    chunks = (lax.axis_index("dev") ^ jnp.arange(4)).astype(jnp.int32)
    pair = [out((2, size, half), F32), out((2, size, half), BF)]
    keep_a, send_a, keep_b, send_b = call(
        functools.partial(halving_kernel, len(shares)),
        None,
        [SMEM] + [VMEM] * (2 * len(shares)),
        [VMEM] * 4,
        pair * 2,
        deps=before,
    )(chunks, *[own for own, _ in shares], *[got for _, got in shares])
    got_a, got_b = dev_send(send_a, 1), dev_send(send_b, 2)
    one = [out((size, half), F32), out((size, half), BF)]
    mine_a, next_a, mine_b, next_b = call(
        halving_add_kernel, None, [VMEM] * 4, [VMEM] * 4, one * 2
    )(keep_a, got_a, keep_b, got_b)
    last_a, last_b = dev_send(next_a, 2), dev_send(next_b, 1)
    total = call(
        halving_total_kernel,
        None,
        [VMEM] * 4,
        [VMEM] * 2,
        [out((size, 2 * half), F32), out((size, 2 * half), BF)],
        deps=deps,
    )(mine_a, last_a, mine_b, last_b)
    return total, [last_a, last_b]


def dev_all(total, deps=()):
    (sent,) = after([total.astype(BF)], *deps)
    return [dev_send(sent, m) for m in range(1, lax.axis_size("dev"))]


def widen(whole, pieces, deps=()):
    rows = whole.shape[0]
    shapes = [(w, rows) if turned else (rows, w) for _, w, turned in pieces]
    return call(
        functools.partial(widen_kernel, pieces),
        None,
        [VMEM],
        [VMEM] * len(pieces),
        [out(shape, F32) for shape in shapes],
        deps=deps,
    )(whole)


def assemble(total, others, pieces, deps=()):
    size, blocks = total.shape[0], 1 + len(others)
    owners = jnp.stack([lax.axis_index("dev")] + [dev_giver(m) for m in range(1, blocks)])
    shapes = [(w, size * blocks) if turned else (size * blocks, w) for _, w, turned in pieces]
    widest = max([w for _, w, turned in pieces if turned], default=128)
    return call(
        functools.partial(assemble_kernel, blocks, pieces),
        None,
        [SMEM] + [VMEM] * blocks,
        [VMEM] * len(pieces),
        [out(shape, F32) for shape in shapes],
        [pltpu.VMEM((size * blocks, widest), F32)],
        deps,
    )(owners.astype(jnp.int32), total, *others)


def per_device(
    tokens,
    norm_gain,
    w_query,
    key_projection,
    value_projection,
    query_gain,
    key_gain,
    w_out,
    ffn_gain,
    w_gate,
    w_up,
    w_down,
    cotangent,
    sequence,
    position,
):
    rows, piece = tokens.shape
    count = lax.axis_size("gx")
    peers = lax.axis_size("gy")
    width = piece * count
    head = query_gain.shape[0]
    q_cols, kv_cols, hidden_units = w_query.shape[1], key_projection.shape[1], w_gate.shape[1]
    gx, gy = lax.axis_index("gx"), lax.axis_index("gy")
    tile = min(256, rows)
    small_tile = min(128, rows)
    grid = (rows // tile,)

    def lies_at(block):
        if peers == 2 and count % 2 == 0:
            half = count // 2
            return ((block // half) ^ gy) * (half * piece) + (block % half) * piece
        return block * piece

    offsets = jnp.stack(
        [lies_at((gx - s) % count) for s in range(count)]
        + [lies_at((gx + s) % count) for s in range(count)]
    ).astype(jnp.int32)

    below = jnp.concatenate(
        [norm_gain[None], ffn_gain[None], jnp.zeros((14, piece), tokens.dtype)], axis=0
    )
    token_pieces = pieces_of(jnp.concatenate([tokens, below], axis=0))
    gain_block = pl.BlockSpec((16, piece), lambda i: (rows // 16, 0))
    query_parts, key_w_parts, value_w_parts = (
        gather_width(w, 0) for w in (w_query, key_projection, value_projection)
    )
    out_w_parts, down_parts = gather_width(w_out, 1), gather_width(w_down, 1)
    gate_parts, up_parts = gather_width(w_gate, 0), gather_width(w_up, 0)
    halves = len(gate_parts)

    lane = jnp.arange(head)
    rates = (THETA ** (-((lane % (head // 2)).astype(F32) * 2.0) / head))[None, :]
    if peers == 2:
        row_info, col_info, cosine, sine = call(
            prepare_kernel,
            None,
            [VMEM] * 3,
            [VMEM] * 4,
            [out((8, rows), F32), out((8, rows), F32), out((rows, head), F32), out((rows, head), F32)],
        )(sequence[None], position[None], rates)
    else:
        all_seq, all_pos = sequence.reshape(peers, rows), position.reshape(peers, rows)
        own_seq = lax.dynamic_index_in_dim(all_seq, gy, 0, False)
        own_pos = lax.dynamic_index_in_dim(all_pos, gy, 0, False)
        row_info = jnp.concatenate(
            [own_seq[None], own_pos[None], jnp.zeros((6, rows), jnp.int32)], axis=0
        ).astype(F32)
        col_info = jnp.stack([all_seq, all_pos], axis=-1).astype(F32)
        phase = own_pos.astype(F32)[:, None] * rates
        cosine = jnp.cos(phase)
        sine = jnp.sin(phase) * jnp.where(lane < head // 2, -1.0, 1.0)[None, :]
    q_scale = query_gain.astype(F32)[None]
    k_scale = key_gain.astype(F32)[None]

    def whole(parts):
        return [same_block(p.shape) for p in parts]

    normed_one, scale_one, query_lin, key_lin, query_bf, key_bf, value_bf = call(
        functools.partial(qkv_kernel, count, halves, head),
        grid,
        [SMEM]
        + [rows_block(tile, piece)] * count
        + [gain_block] * count
        + whole(query_parts + key_w_parts + value_w_parts)
        + [same_block((1, head))] * 2
        + [rows_block(tile, head)] * 2,
        [
            rows_block(tile, width),
            rows_block(tile, 1),
            rows_block(tile, q_cols),
            rows_block(tile, kv_cols),
            rows_block(tile, q_cols),
            rows_block(tile, kv_cols),
            rows_block(tile, kv_cols),
        ],
        [
            out((rows, width), BF),
            out((rows, 1), F32),
            out((rows, q_cols), F32),
            out((rows, kv_cols), F32),
            out((rows, q_cols), BF),
            out((rows, kv_cols), BF),
            out((rows, kv_cols), BF),
        ],
        deps=[row_info, col_info],
    )(
        offsets, *token_pieces, *token_pieces, *query_parts, *key_w_parts, *value_w_parts,
        q_scale, k_scale, cosine, sine,
    )
    if peers == 2:
        keys = [key_bf, shifted(key_bf, "gy", 1)]
        values = [value_bf, shifted(value_bf, "gy", 1)]
    else:
        keys = [lax.all_gather(key_bf, "gy", axis=0)]
        values = [lax.all_gather(value_bf, "gy", axis=0)]
    (late_cotangent,) = after([cotangent], *token_pieces[1:], cosine, offsets)
    cot_pieces = [cotangent] + pieces_of(late_cotangent)[1:]

    mixed, attended, logs = call(
        functools.partial(attend_kernel, head, small_tile, peers),
        None,
        [VMEM] * (3 + 2 * len(keys)),
        [VMEM] * 3,
        [
            out((rows, q_cols), BF),
            out((q_cols, rows), F32),
            out((max(8, q_cols // head), rows), F32),
        ],
        deps=[cot_pieces[1], cot_pieces[-1]],
    )(query_bf, row_info, col_info, *keys, *values)

    split_out = [out((rows, piece), F32)] + [out((rows, piece), BF)] * (count - 1)

    def split_dot(left, weights, *deps):
        return call(
            functools.partial(split_dot_kernel, count, halves),
            grid,
            [SMEM, rows_block(tile, left.shape[1])] + whole(weights),
            [rows_block(tile, piece)] * count,
            split_out,
            deps=deps,
        )(offsets, left, *weights)

    out_parts = split_dot(mixed, out_w_parts, *cot_pieces[1:])
    inputs = tokens.astype(F32)
    hidden = inputs + piece_sum(out_parts[0], out_parts[1:])

    cot_whole, grad_product, normed_turned, cot_turned, cot_sent = call(
        functools.partial(cot_kernel, count),
        grid,
        [SMEM] + [rows_block(tile, piece)] * count + [rows_block(tile, width)] + whole(down_parts),
        [
            rows_block(tile, width),
            rows_block(tile, hidden_units),
            pl.BlockSpec((width, tile), lambda i: (0, i)),
            pl.BlockSpec((width // 2, tile), lambda i: (0, i)),
            pl.BlockSpec((width // 2, tile), lambda i: (0, i)),
        ],
        [out((rows, width), BF), out((rows, hidden_units), F32), out((width, rows), BF)]
        + [out((width // 2, rows), BF)] * 2,
    )(offsets, *cot_pieces, normed_one, *down_parts)

    hidden_pieces = pieces_of(hidden.astype(BF))
    *grad_parts, normed_two, scale_two, product, deltas, normed_sent = call(
        functools.partial(ffn_kernel, count, halves),
        grid,
        [SMEM]
        + [rows_block(tile, piece)] * count
        + [gain_block] * count
        + whole(gate_parts + up_parts)
        + [rows_block(tile, hidden_units)],
        [rows_block(tile, piece)] * count
        + [rows_block(tile, width), rows_block(tile, 1), rows_block(tile, hidden_units)]
        + [rows_block(tile, 3 * hidden_units), rows_block(tile, width // 2)],
        split_out
        + [out((rows, width), BF), out((rows, 1), F32), out((rows, hidden_units), BF)]
        + [out((rows, 3 * hidden_units), BF), out((rows, width // 2), BF)],
    )(offsets, *hidden_pieces, *token_pieces, *gate_parts, *up_parts, grad_product)

    grad_got = [shifted(p, "gx", s) for s, p in enumerate(grad_parts[1:], 1)]
    grad_normed_two = grad_parts[0]
    for part in grad_got:
        grad_normed_two = grad_normed_two + part.astype(F32)
    grad_pieces = pieces_of(grad_normed_two.astype(BF))
    result_parts = split_dot(product, down_parts, *grad_got)
    blocks = lax.axis_size("dev")
    if peers == 2:
        half = pl.BlockSpec((rows, width // 4), lambda i: (0, i))
        turned_half = pl.BlockSpec((width // 4, rows), lambda i: (i, 0))
        ffn_share = call(
            ffn_share_kernel,
            (2,),
            [half, half, turned_half, turned_half] + [same_block(deltas.shape)] * 2,
            rows_block(width // 4, 3 * hidden_units),
            out((width // 2, 3 * hidden_units), BF),
        )(
            normed_two, shifted(normed_sent, "gy", 1), cot_turned, shifted(cot_sent, "gy", 1),
            deltas, shifted(deltas, "gy", 1),
        )
        (ffn_share,) = after([ffn_share], *grad_got)
    else:
        ffn_share, _ = weight_grads(
            [
                (normed_two, [deltas[:, : 2 * hidden_units]]),
                (cot_whole, [deltas[:, 2 * hidden_units :]]),
            ]
        )
        ffn_share = ffn_share.reshape(-1, 3 * hidden_units)
    ffn_chunk = lax.psum_scatter(ffn_share, "dev", scatter_dimension=0, tiled=True)

    late_parts = after(result_parts[1:], *grad_pieces[1:])
    branch, grad_mixed, inner_two = call(
        functools.partial(branch_kernel, count, halves),
        grid,
        [SMEM]
        + [rows_block(tile, piece)] * (2 * count)
        + [gain_block] * count
        + [rows_block(tile, 1), rows_block(tile, width)]
        + whole(out_w_parts),
        [rows_block(tile, width), rows_block(tile, q_cols), rows_block(tile, 1)],
        [out((rows, width), BF), out((rows, q_cols), BF), out((rows, 1), F32)],
        deps=[late_parts[0]],
    )(
        offsets, *hidden_pieces, *grad_pieces, *token_pieces, scale_two, cot_whole, *out_w_parts
    )

    result_got = [shifted(p, "gx", s) for s, p in enumerate(late_parts, 1)]
    result = hidden + result_parts[0]
    for part in result_got:
        result = result + part.astype(F32)
    out_own, out_got = weight_grads([(branch, [mixed])])

    ffn_low, grad_query_lin, query_gain_part, *kv_parts = call(
        functools.partial(attend_back_kernel, head, small_tile, peers),
        None,
        [VMEM] * (10 + 2 * len(keys)) + [ANY],
        [ANY] + [VMEM] * (2 + 2 * len(keys)),
        [out(ffn_chunk.shape, BF), out((rows, q_cols), BF), out((1, head), F32)]
        + [out(k.shape, BF) for k in keys + values],
        [pltpu.VMEM((peers, rows, kv_cols), F32), pltpu.VMEM((peers, rows, kv_cols), F32)],
        deps=[out_own, result_got[0], result_got[-1]],
        aliases={10 + 2 * len(keys): 0},
    )(
        grad_mixed, query_bf, query_lin, row_info, col_info, attended, logs,
        q_scale, cosine, sine, *keys, *values, ffn_chunk,
    )
    ffn_sum = lax.all_gather(ffn_low, "dev", axis=0, tiled=True)
    if peers == 2:
        key_terms = [kv_parts[0], shifted(kv_parts[1], "gy", 1)]
        value_terms = [kv_parts[2], shifted(kv_parts[3], "gy", 1)]
    else:
        share = lambda a: lax.psum_scatter(a, "gy", scatter_dimension=0, tiled=True)[0]
        key_terms, value_terms = [share(kv_parts[0])], [share(kv_parts[1])]

    fused = peers == 2
    shares = [out(out_own.shape[:2] + (q_cols + 2 * kv_cols,), BF)] * 2 if fused else []
    *last_outs, grad_key_lin, grad_value_lin = call(
        functools.partial(lin_back_kernel, count, halves, head, len(key_terms), fused),
        None,
        [SMEM] + [VMEM] * (8 + 2 * len(key_terms) + 3 * halves + fused),
        [VMEM] * (count + 2 + len(shares)),
        shares
        + [out((rows + 16, piece), p.dtype) for p in split_out]
        + [out((rows, kv_cols), BF)] * 2,
    )(
        offsets, grad_query_lin, query_lin, key_lin, value_bf, query_gain_part,
        *key_terms, *value_terms, k_scale, cosine, sine,
        *query_parts, *key_w_parts, *value_w_parts, *([normed_turned] if fused else []),
    )
    last_parts = last_outs[len(shares) :]
    last_got = [shifted(p, "gx", s) for s, p in enumerate(last_parts[1:], 1)]
    if fused:
        last_share = last_outs[0], shifted(last_outs[1], "gy", 1)
    else:
        last_share = weight_grads(
            [(normed_turned, [grad_query_lin, grad_key_lin, grad_value_lin])]
        )
    last_shares = [last_share, (out_own, out_got)]
    if fused and blocks == 4:
        (last_total, last_low), dev_got = halving_total(last_shares, [], last_got)
    else:
        last_chunks = share_chunks(last_shares)
        last_total, dev_got = dev_total(last_chunks)
        last_low = last_total.astype(BF)
    last_others = dev_all(last_low)
    gate_grad, up_grad, down_grad = widen(
        ffn_sum,
        (
            (0, hidden_units, False),
            (hidden_units, hidden_units, False),
            (2 * hidden_units, hidden_units, True),
        ),
        [last_total],
    )
    cuts = (0, q_cols, q_cols + kv_cols, q_cols + 2 * kv_cols)
    query_grad, key_grad, value_grad, out_grad = assemble(
        last_total,
        last_others,
        (
            (cuts[0], q_cols, False),
            (cuts[1], kv_cols, False),
            (cuts[2], kv_cols, False),
            (cuts[3], q_cols, True),
        ),
        [down_grad],
    )

    grad_inputs, gain_part = call(
        functools.partial(final_kernel, count),
        None,
        [VMEM] * (count + 7),
        [VMEM] * 2,
        [out((rows, piece), F32), out((8, piece), F32)],
        deps=[last_low],
    )(
        last_parts[0], *last_got, token_pieces[0], cotangent, hidden, grad_normed_two,
        scale_one, scale_two, inner_two,
    )
    if peers == 2:
        last = small_sum(small_sum(gain_part, "gy"), "dev")
    else:
        last = lax.psum(gain_part, ("dev", "gy"))
    return (
        result.astype(BF),
        grad_inputs,
        last[0],
        query_grad,
        key_grad,
        value_grad,
        last[2, :head],
        last[2, head : 2 * head],
        out_grad,
        last[1],
        gate_grad,
        up_grad,
        down_grad,
    )


def solution(mesh):
    wide = P(("dev", "gy"), "gx")
    weight, back = P("gy", "gx"), P("gx", "gy")
    return jax.shard_map(
        per_device,
        mesh=mesh,
        in_specs=(
            wide, P("gx"), weight, weight, weight, P(), P(), back, P("gx"), weight, weight, back,
            wide, P("dev"), P("dev"),
        ),
        out_specs=(
            wide, wide, P("gx"), weight, weight, weight, P(), P(), back, P("gx"), weight, weight,
            back,
        ),
        check_vma=False,
    )
```
